512 devices in a mesh: tm: 8 (over z_hi, y), space: 64 (over x, z_lo, core).
Axes of the slice: x: 4, y: 4, z: 16 (z_hi: 2, z_lo: 8; z = z_hi * 8 + z_lo), core: 2. Of those that a mesh axis runs over, the one named last changes fastest.
Arguments:
- noisy_state: float32 [32, 2, 1024, 256], P('tm', None, 'space'), may hold values from -6 to 6
- fresh_noise: float32 [32, 2, 1024, 256], P('tm', None, 'space'), may hold values from -6 to 6
- level_index: int32 [1], replicated, may hold values from 1 to 31
- station_obs: float32 [32, 2, 8192], P('tm', None, 'space'), may hold values from -6 to 6
- obs_variance: float32 [8192], P('space'), may hold values from 0.05 to 0.5
- station_owner: int32 [8192, 1], P('space'), may hold values from 0 to 63; in each aligned block of 128 rows (0 to 127, 128 to 255, ...) at most 8 rows name the same one
- station_cell: int32 [8192], P('space'), may hold values from 0 to 4095
- conv_in: bfloat16 [3, 64, 48], replicated, may hold values from -0.5 to 0.5
- conv_mid: bfloat16 [3, 64, 192], replicated, may hold values from -0.25 to 0.25
- conv_res: bfloat16 [3, 64, 192], replicated, may hold values from -0.25 to 0.25
- conv_out: bfloat16 [3, 16, 192], replicated, may hold values from -0.25 to 0.25
- in_bias: float32 [64], replicated, may hold values from -3 to 3
- noise_embed: float32 [64], replicated, may hold values from -3 to 3
- norm_gain: float32 [64], replicated, may hold values from 0.5 to 2
Outputs:
- next_state: float32 [32, 2, 1024, 256], P('tm', None, 'space')
The draws below stay inside these ranges and needn't reach their ends.
Inputs may be any that keep to these rules, and one draw needn't show every extreme that they name: `station_owner`: among the stations of one device (each aligned block of 128 stations) at most 8 have the same owner strip; every strip owns some station.
All inputs are finite; a program needn't handle non-finite values.
Results may differ from the reference program's by a relative error of at most 0.0023.
Values may be sent and summed in bfloat16 or wider, within the bound.
No kernel may reach another device: no remote copies, remote signals or barrier semaphores. Data moves between devices by JAX's collectives and lax.ppermute only.
A program may use at most 64 MiB of HBM per device.

```python
import math
import jax
import jax.numpy as jnp
import numpy as np
from jax import lax

C = 64
WIN = 8
LEVELS = 32
ROWS = 16
COLS = 256
STA_DEV = 128
STRIDE = 4
CHAN = 16
TIMES = 32
NY = 1024
NX = 256
STATIONS = 8192
CAP = 8
N_SPACE = 64


def plant(values, stream_key, least, high):
    longest = values.shape.index(max(values.shape))
    spots = []
    for shift in (0, 1):
        where = [jax.random.randint(jax.random.fold_in(stream_key, axis), (), 0, length) for axis, length in enumerate(values.shape)]
        where[longest] = (where[longest] + shift) % values.shape[longest]
        spots.append(tuple(where))
    return values.at[spots[0]].set(least).at[spots[1]].set(high)


def block_levels(stream_key, extent, pieces, least, top_value):
    level, own = 1.0, jax.random.fold_in(stream_key, 6)
    for axis_at, shards_of in pieces:
        draws = jnp.exp(jax.random.uniform(jax.random.fold_in(own, axis_at), (shards_of,), jnp.float32, least / len(pieces), top_value / len(pieces)))
        level = level * jnp.repeat(draws, extent[axis_at] // shards_of).reshape([-1 if axis == axis_at else 1 for axis in range(len(extent))])
    return level


def routed_block(key, own, number, rows, amount, top, bound, skew):
    order = jax.random.permutation(key, amount)
    packed, usual = portions_of(amount, rows * top, bound, skew, True), portions_of(amount, rows * top, bound, skew, False)
    places = jnp.arange(amount)

    def named(sizes, turn):
        used = int((sizes > 0).sum())
        fixed = max(1, used // 4)
        shifted = fixed + (places - fixed + turn * (used - fixed)) % max(1, amount - fixed)
        return jnp.zeros((amount,), jnp.int32).at[order[jnp.where(places < fixed, places, shifted)]].set(jnp.asarray(sizes, jnp.int32))

    sizes = jnp.where(number % 4 == 0, named(packed, number // 4), named(usual, number - number // 4 - 1))
    mixed = jax.random.permutation(jax.random.fold_in(own, 3), amount)
    donor, taker = mixed[0:amount // 2 * 2:2], mixed[1:amount // 2 * 2:2]
    room = jnp.minimum(sizes[donor] - 1, bound - sizes[taker]) // 2
    room = jnp.where((donor == order[0]) | (taker == order[0]) | (sizes[taker] == 0), 0, jnp.maximum(room, 0))
    shifted = jax.random.randint(jax.random.fold_in(own, 4), (amount // 2,), 0, 1 << 20) % (room + 1)
    sizes = sizes.at[donor].add(-shifted).at[taker].add(shifted)
    items = jnp.searchsorted(jnp.cumsum(sizes), jnp.arange(rows * top), side="right").astype(jnp.int32)
    listing = items.reshape(top, rows).T
    listing = listing[jax.random.permutation(jax.random.fold_in(own, 1), rows)]
    turn = jax.random.randint(jax.random.fold_in(own, 2), (rows, 1), 0, top)
    return jnp.take_along_axis(listing, (jnp.arange(top)[None, :] + turn) % top, axis=1)


def portions_of(count, total, bound, skew, full):
    weights = [(1 << 20) // math.isqrt(grade ** skew) + 1 for grade in range(1, count + 1)]
    largest = bound if full else min(bound, max(-(-total // count), total * weights[0] // sum(weights)))
    least = 1 if total - largest >= count - 1 else 0
    holding, rest = [largest] + [least] * (count - 1), total - largest - least * (count - 1)
    while rest > 0:
        movable = [i for i in range(1, count) if holding[i] < largest] or [i for i in range(1, count) if holding[i] < bound]
        mass, left = sum([weights[i] for i in movable]), rest
        for i in movable:
            addition = min(bound - holding[i], max(1, left * weights[i] // mass), rest)
            holding[i] = holding[i] + addition
            rest = rest - addition
    return np.array(holding)


def normal_values(key, extent, deviation, limit, shards=(), held_as=jnp.bfloat16):
    values = jax.random.normal(key, extent, jnp.float32) * deviation
    if len(shards) > 0:
        values = block_levels(key, extent, shards, -0.22, 0.18) * values
    return jnp.clip(values, min=-limit, max=limit).astype(held_as)


def setup_inputs(seed: int = 0) -> dict:
    splits = jax.random.split(jax.random.key(seed), 15)
    noisy_state = normal_values(splits[0], (TIMES, 2, NY, NX), 1.0, 6.0, ((0, 8), (2, 64)), jnp.float32)
    fresh_noise = normal_values(splits[1], (TIMES, 2, NY, NX), 1.0, 6.0, ((0, 8), (2, 64)), jnp.float32)
    level_index = jax.random.randint(splits[2], (1,), 1, LEVELS).astype(jnp.int32)
    station_obs = normal_values(splits[3], (TIMES, 2, STATIONS), 1.0, 6.0, ((0, 8), (2, 64)), jnp.float32)
    obs_variance = jnp.clip(jnp.exp(math.log(0.5) - 2.3025851 * jax.random.uniform(splits[4], (STATIONS,), jnp.float32) ** block_levels(splits[4], (STATIONS,), ((0, 64),), -0.2, 0.2)), 0.05, 0.5)
    station_owner_keys = jax.random.split(jax.random.fold_in(splits[5], 1), STATIONS // STA_DEV)
    station_owner_turns = jax.random.permutation(jax.random.fold_in(splits[5], 3), STATIONS // STA_DEV)
    station_owner = jax.vmap(lambda own, number: routed_block(jax.random.fold_in(splits[5], 2), own, number, STA_DEV, N_SPACE, 1, CAP, 2))(station_owner_keys, station_owner_turns).reshape((STATIONS, 1))
    station_cell = plant(jax.random.randint(splits[6], (STATIONS,), 0, ROWS * COLS), jax.random.fold_in(splits[6], 1), 0, (ROWS * COLS) - 1).astype(jnp.int32)
    conv_in = normal_values(splits[7], (3, C, 3 * CHAN), (9 * CHAN) ** -0.5, 0.5)
    conv_mid = normal_values(splits[8], (3, C, 3 * C), (9 * C) ** -0.5, 0.25)
    conv_res = normal_values(splits[9], (3, C, 3 * C), (9 * C) ** -0.5, 0.25)
    conv_out = normal_values(splits[10], (3, CHAN, 3 * C), (9 * C) ** -0.5, 0.25)
    in_bias = normal_values(splits[11], (C,), 0.5, 3.0, (), jnp.float32)
    noise_embed = normal_values(splits[12], (C,), 0.5, 3.0, (), jnp.float32)
    norm_gain = jnp.clip(jnp.exp(jax.random.uniform(splits[13], (C,), jnp.float32, math.log(0.5), math.log(2.0))), 0.5, 2.0)
    return dict(noisy_state=noisy_state, fresh_noise=fresh_noise, level_index=level_index, station_obs=station_obs, obs_variance=obs_variance, station_owner=station_owner, station_cell=station_cell, conv_in=conv_in, conv_mid=conv_mid, conv_res=conv_res, conv_out=conv_out, in_bias=in_bias, noise_embed=noise_embed, norm_gain=norm_gain)


def scale_at(level):
    return 0.3 * jnp.exp(jnp.log(5.0) * level.astype(jnp.float32) / (LEVELS - 1))

def conv_full(weight, field):
    inputs = field.shape[0]
    moving = field.astype(jnp.float32)
    total = jnp.zeros((weight.shape[1],) + field.shape[1:], jnp.float32)
    for row_tap in range(3):
        for col_tap in range(3):
            moved = jnp.roll(moving, (1 - row_tap, 1 - col_tap), axis=(1, 2))
            kernel = weight[row_tap][:, col_tap * inputs:(col_tap + 1) * inputs].astype(jnp.float32)
            total = total + jnp.einsum('oc,cyx->oyx', kernel, moved)
    return total

def score_full(window_in, conv_in, conv_mid, conv_res, conv_out, bias, norm_gain):
    first = jax.nn.silu(conv_full(conv_in, window_in) + bias[:, None, None]).astype(jnp.bfloat16)
    middle = conv_full(conv_mid, first)
    normed = middle * lax.rsqrt(lax.optimization_barrier(jnp.mean(middle * middle, axis=0, keepdims=True)) + 1e-05) * norm_gain[:, None, None]
    second = jax.nn.silu(normed).astype(jnp.bfloat16)
    branch = jax.nn.silu(conv_full(conv_res, second))
    third = (first.astype(jnp.float32) + branch).astype(jnp.bfloat16)
    return conv_full(conv_out, third)

def reference(noisy_state, fresh_noise, level_index, station_obs, obs_variance, station_owner, station_cell, conv_in, conv_mid, conv_res, conv_out, in_bias, noise_embed, norm_gain):
    noise_scale = scale_at(level_index[0])
    next_scale = scale_at(level_index[0] - 1)
    bias = in_bias + noise_embed * jnp.log(10.0 * noise_scale)
    scaled = (noisy_state / jnp.sqrt(1.0 + noise_scale * noise_scale)).astype(jnp.bfloat16)
    window_total = TIMES // STRIDE - 1

    def accumulate(summed, window):
        start_step = (window * STRIDE).astype(jnp.int32)
        window_in = lax.dynamic_slice_in_dim(scaled, start_step, WIN, 0).reshape(CHAN, NY, NX)
        result = score_full(window_in, conv_in, conv_mid, conv_res, conv_out, bias, norm_gain).reshape(WIN, 2, NY, NX)
        current = lax.dynamic_slice_in_dim(summed, start_step, WIN, 0)
        return (lax.dynamic_update_slice_in_dim(summed, current + result, start_step, 0), None)
    summed, unused = lax.scan(accumulate, jnp.zeros((TIMES, 2, NY, NX), jnp.float32), jnp.arange(window_total, dtype=jnp.int32))
    moment = jnp.arange(TIMES, dtype=jnp.int32)
    cover = jnp.where((moment < STRIDE) | (moment >= TIMES - STRIDE), 1.0, 2.0).astype(jnp.float32)
    estimate = noisy_state - noise_scale * (summed / cover[:, None, None, None])
    owners = station_owner[:, 0]
    row_of = (owners * ROWS + station_cell // COLS).astype(jnp.int32)
    col_of = (station_cell % COLS).astype(jnp.int32)
    seen = estimate[:, :, row_of, col_of]
    misfit = (station_obs - seen) / (obs_variance + noise_scale * noise_scale)
    pull = jnp.zeros_like(estimate).at[:, :, row_of, col_of].add(misfit)
    return estimate + noise_scale * noise_scale * pull + next_scale * fresh_noise
```

```python
import jax
import jax.numpy as jnp
from jax import lax
from jax.experimental import pallas as pl
from jax.experimental.pallas import tpu as pltpu
from jax.sharding import PartitionSpec as P

LEVELS = 32
BF = jnp.bfloat16
F32 = jnp.float32
GROUP = 2
OUT_GROUP = 4
VM = pl.BlockSpec(memory_space=pltpu.VMEM)
SM = pl.BlockSpec(memory_space=pltpu.SMEM)


def scale_at(level):
    return 0.3 * jnp.exp(jnp.log(5.0) * level.astype(jnp.float32) / (LEVELS - 1))


def rolled(x, k):
    return pltpu.roll(x, k % x.shape[1], 1)


def parts_of(v):
    high = v.astype(BF)
    rest = v - high.astype(F32)
    middle = rest.astype(BF)
    low = (rest - middle.astype(F32)).astype(BF)
    return high, middle, low


def silu_half(h):
    return h + h * jnp.tanh(h)


def pack_body(scal, obs, var, owner, cell, out):
    count = obs.shape[2]
    slots = out.shape[0]
    own_col = owner[...]
    row = lax.broadcasted_iota(jnp.int32, (count, count), 0)
    col = lax.broadcasted_iota(jnp.int32, (count, count), 1)
    own_row = jnp.sum(jnp.where(row == col, own_col, 0).astype(F32), axis=0, keepdims=True)
    same = (own_col.astype(F32) == own_row) & (row < col)
    rank = jnp.sum(jnp.where(same, 1.0, 0.0), axis=0, keepdims=True)
    slot = (own_row * 8.0 + rank).astype(jnp.int32)
    weight = 1.0 / (var[...] + scal[0])
    values = jnp.concatenate([obs[k] for k in range(obs.shape[0])], axis=0) * weight
    spot = cell[...]
    extra = [weight, (spot // 256).astype(F32), (spot % 256).astype(F32)]
    spare = jnp.zeros((128 - values.shape[0] - len(extra), count), F32)
    table = jnp.concatenate([values] + extra + [spare], axis=0)
    hot = jnp.where(
        lax.broadcasted_iota(jnp.int32, (slots, count), 0) == slot, 1.0, 0.0
    ).astype(BF)
    total = None
    for part in parts_of(table):
        piece = lax.dot_general(
            hot, part, (((1,), (1,)), ((), ())), preferred_element_type=F32
        )
        total = piece if total is None else total + piece
    out[...] = total


def pack(scal, obs, var, owner, cell):
    return pl.pallas_call(
        pack_body,
        out_shape=jax.ShapeDtypeStruct((512, 128), F32),
        in_specs=[SM, VM, VM, VM, VM],
        out_specs=VM,
        cost_estimate=pl.CostEstimate(flops=50_000_000, bytes_accessed=400_000, transcendentals=0),
    )(scal, obs, var, owner, cell)


def finish_body(scal, noisy, fresh, den, got, out):
    slots = got.shape[0]
    table = got[...].T
    masks = (
        lax.broadcasted_iota(jnp.int32, (16, slots), 0) == table[9:10].astype(jnp.int32)
    )
    cols = jnp.where(
        lax.broadcasted_iota(jnp.int32, (256, slots), 0) == table[10:11].astype(jnp.int32),
        1.0,
        0.0,
    ).astype(BF)
    left = jnp.concatenate(
        [jnp.where(masks, table[v : v + 1], 0.0) for v in range(9)], axis=0
    )
    total = None
    for part in parts_of(left):
        piece = lax.dot_general(
            part, cols, (((1,), (1,)), ((), ())), preferred_element_type=F32
        )
        total = piece if total is None else total + piece
    square, after, scale = scal[0], scal[1], scal[2]
    weight = total[128:144]
    for v in range(8):
        estimate = noisy[v] - scale * den[v]
        pull = total[v * 16 : (v + 1) * 16] - estimate * weight
        out[v] = estimate + square * pull + after * fresh[v]


def finish(scal, noisy, fresh, den, got):
    return pl.pallas_call(
        finish_body,
        out_shape=jax.ShapeDtypeStruct((8, 16, 256), F32),
        in_specs=[SM, VM, VM, VM, VM],
        out_specs=VM,
        cost_estimate=pl.CostEstimate(flops=100_000_000, bytes_accessed=800_000, transcendentals=0),
    )(scal, noisy, fresh, den, got)


def conv_body(par, own, t1, t2, m1, m2, w1, wm, wr, wo, b1, gain, out, x1, x2, x3, x4):
    even_t = par[0] == 1
    even_s = par[1] == 1

    def shifts(v):
        b = v.astype(BF)
        left, right = b[:, :256], b[:, 256:]
        return (
            jnp.concatenate([rolled(left, 1), rolled(right, 1)], 1),
            b,
            jnp.concatenate([rolled(left, -1), rolled(right, -1)], 1),
        )

    def row_in(o, a, b, y):
        o, a, b = o.astype(F32), a.astype(F32), b.astype(F32)
        before = jnp.where(even_t, b, a)
        later = jnp.where(even_t, a, b)
        tap_b, tap_o, tap_l = [(rolled(z, 1), z, rolled(z, -1)) for z in (before, o, later)]
        left = jnp.concatenate([z for k in range(3) for z in (tap_b[k], tap_o[k])], 0)
        right = jnp.concatenate([z for k in range(3) for z in (tap_o[k], tap_l[k])], 0)
        x1[y * 48 : (y + 1) * 48, :256] = left.astype(BF)
        x1[y * 48 : (y + 1) * 48, 256:] = right.astype(BF)

    for y in range(16):
        row_in(own[y], t1[y], t2[y], 4 + y)
    for y in range(4):
        u, v = m1[y].astype(F32), m2[y].astype(F32)
        top = jnp.where(even_s, v, u)
        low = jnp.where(even_s, u, v)
        row_in(top[:8], top[8:16], top[16:], y)
        row_in(low[:8], low[8:16], low[16:], 20 + y)

    for g in range(8):
        y0 = min(3 * g, 19)
        acc = jnp.dot(w1[...], x1[y0 * 48 : y0 * 48 + 240, :], preferred_element_type=F32)
        for r in range(3 * g - y0, 3):
            taps = shifts(silu_half(acc[r * 64 : (r + 1) * 64] + b1[...]))
            for k in range(3):
                at = (y0 + r) * 192 + k * 64
                x2[at : at + 64, :] = taps[k]

    for g in range(20 // GROUP):
        y0 = g * GROUP
        acc = jnp.dot(
            wm[...], x2[y0 * 192 : (y0 + GROUP + 2) * 192, :], preferred_element_type=F32
        )
        for r in range(GROUP):
            m = acc[r * 64 : (r + 1) * 64]
            mean = jnp.sum(m * m, axis=0, keepdims=True) * (1 / 64)
            taps = shifts(silu_half(m * lax.rsqrt(mean + 1e-05) * gain[...]))
            for k in range(3):
                at = (y0 + r) * 192 + k * 64
                x3[at : at + 64, :] = taps[k]

    for g in range(18 // GROUP):
        y0 = g * GROUP
        acc = jnp.dot(
            wr[...], x3[y0 * 192 : (y0 + GROUP + 2) * 192, :], preferred_element_type=F32
        )
        for r in range(GROUP):
            y = y0 + r
            f = x2[(y + 2) * 192 + 64 : (y + 2) * 192 + 128, :].astype(F32)
            third = (f + silu_half(acc[r * 64 : (r + 1) * 64])).astype(BF)
            x4[y * 128 : y * 128 + 64, :] = third[:, :256]
            x4[y * 128 + 64 : y * 128 + 128, :] = third[:, 256:]

    size = OUT_GROUP * 8
    for g in range(16 // OUT_GROUP):
        y0 = g * OUT_GROUP
        acc = jnp.dot(
            wo[...], x4[y0 * 128 : (y0 + OUT_GROUP + 2) * 128, :], preferred_element_type=F32
        )
        res = rolled(acc[:size], 1) + acc[size : 2 * size] + rolled(acc[2 * size :], -1)
        for r in range(OUT_GROUP):
            out[:, y0 + r, :] = res[r * 8 : (r + 1) * 8]


def convs(par, own, t1, t2, m1, m2, w1, wm, wr, wo, b1, gain):
    return pl.pallas_call(
        conv_body,
        out_shape=jax.ShapeDtypeStruct((8, 16, 256), F32),
        in_specs=[SM] + [VM] * 11,
        out_specs=VM,
        scratch_shapes=[
            pltpu.VMEM((24 * 48, 512), BF),
            pltpu.VMEM((22 * 192, 512), BF),
            pltpu.VMEM((20 * 192, 512), BF),
            pltpu.VMEM((18 * 128, 256), BF),
        ],
        compiler_params=pltpu.CompilerParams(vmem_limit_bytes=40 * 2**20),
        cost_estimate=pl.CostEstimate(
            flops=8_000_000_000, bytes_accessed=1_000_000, transcendentals=2_000_000
        ),
    )(par, own, t1, t2, m1, m2, w1, wm, wr, wo, b1, gain)


def banded(weight, rows, factor):
    taps, outs, depth = weight.shape
    flat = (weight.astype(F32) * factor).astype(BF).transpose(1, 0, 2).reshape(outs, taps * depth)
    return jnp.concatenate(
        [jnp.pad(flat, ((0, 0), (r * depth, (rows - 1 - r) * depth))) for r in range(rows)], 0
    )


def banded_out(conv_out, coef):
    w = conv_out.reshape(3, 2, 8, 3, 64)
    w = jnp.stack([w[:, 1], w[:, 0]], 0).astype(F32) * coef[:, None, None, None, None]
    w = w.astype(BF).transpose(3, 2, 1, 0, 4).reshape(3, 8, 3 * 128)
    last = OUT_GROUP - 1
    return jnp.concatenate(
        [
            jnp.pad(w[b], ((0, 0), (r * 128, (last - r) * 128)))
            for b in range(3)
            for r in range(OUT_GROUP)
        ],
        0,
    )


def swapped(value, axis, first):
    count = lax.axis_size(axis)
    wrap = axis == "space"
    pairs = []
    for i in range(first, count if wrap else count - 1, 2):
        j = (i + 1) % count
        pairs += [(i, j), (j, i)]
    return lax.ppermute(value, axis, pairs)


def local(
    noisy_state,
    fresh_noise,
    level_index,
    station_obs,
    obs_variance,
    station_owner,
    station_cell,
    conv_in,
    conv_mid,
    conv_res,
    conv_out,
    in_bias,
    noise_embed,
    norm_gain,
):
    noise_scale = scale_at(level_index[0])
    next_scale = scale_at(level_index[0] - 1)
    bias = in_bias + noise_embed * jnp.log(10.0 * noise_scale)
    scal = jnp.stack([noise_scale * noise_scale, next_scale, noise_scale])
    time_rank = lax.axis_index("tm")
    times = lax.axis_size("tm")
    strip = lax.axis_index("space")
    even_t = time_rank % 2 == 0
    even_s = strip % 2 == 0
    par = jnp.stack([even_t, even_s]).astype(jnp.int32)

    noisy = noisy_state.reshape(8, 16, 256)
    own = (noisy / jnp.sqrt(1.0 + noise_scale * noise_scale)).astype(BF).transpose(1, 0, 2)
    t2 = swapped(own, "tm", 1)
    t1 = swapped(own, "tm", 0)

    slots = pack(
        scal,
        station_obs,
        obs_variance.reshape(1, 128),
        station_owner,
        station_cell.reshape(1, 128),
    )
    got = lax.all_to_all(slots.reshape(64, 8, 128), "space", 0, 0, tiled=True).reshape(512, 128)

    edge = jnp.where(even_s, 12, 0)
    both = jnp.concatenate([own, t1, t2], axis=1)
    m2 = swapped(lax.dynamic_slice_in_dim(both, 12 - edge, 4, 0), "space", 1)
    m1 = swapped(lax.dynamic_slice_in_dim(both, edge, 4, 0), "space", 0)

    coef = jnp.stack(
        [
            jnp.where(time_rank == 0, 0.0, jnp.where(time_rank == times - 1, 1.0, 0.5)),
            jnp.where(time_rank == 0, 1.0, jnp.where(time_rank == times - 1, 0.0, 0.5)),
        ]
    )
    den = convs(
        par,
        own,
        t1,
        t2,
        m1,
        m2,
        banded(conv_in, 3, 0.5),
        banded(conv_mid, GROUP, 1.0),
        banded(conv_res, GROUP, 0.5),
        banded_out(conv_out, coef),
        (0.5 * bias)[:, None],
        (0.5 * norm_gain)[:, None],
    )
    result = finish(scal, noisy, fresh_noise.reshape(8, 16, 256), den, got)
    return result.reshape(noisy_state.shape)


def solution(mesh):
    rest = (P(),) * 7
    placed = (
        P("tm", None, "space", None),
        P("tm", None, "space", None),
        P(),
        P("tm", None, "space"),
        P("space"),
        P("space", None),
        P("space"),
    ) + rest
    return jax.shard_map(
        local, mesh=mesh, in_specs=placed, out_specs=P("tm", None, "space", None), check_vma=False
    )
```

```python
import math

import jax
import jax.numpy as jnp
from jax import lax
from jax.experimental import pallas as pl
from jax.experimental.pallas import tpu as pltpu
from jax.sharding import PartitionSpec as P

LEVELS = 32
BF = jnp.bfloat16
F32 = jnp.float32
OUT_GROUP = 4
INNER_COST = 8_000_000_000
VM = pl.BlockSpec(memory_space=pltpu.VMEM)
SM = pl.BlockSpec(memory_space=pltpu.SMEM)
ANY = pl.BlockSpec(memory_space=pl.ANY)


def scale_at(level, shape):
    steps = jnp.full(shape, level, jnp.int32).astype(F32)
    return 0.3 * jnp.exp(math.log(5.0) * steps / (LEVELS - 1))


def rolled(x, k):
    return pltpu.roll(x, k % x.shape[1], 1)


def parts_of(v):
    high = v.astype(BF)
    rest = v - high.astype(F32)
    middle = rest.astype(BF)
    low = (rest - middle.astype(F32)).astype(BF)
    return high, middle, low


def silu_half(h):
    return h + h * jnp.tanh(h)


def column_of(row):
    size = row.shape[1]
    line = lax.broadcasted_iota(jnp.int32, (size, size), 0)
    lane = lax.broadcasted_iota(jnp.int32, (size, size), 1)
    return jnp.sum(jnp.where(line == lane, row, 0.0), axis=1, keepdims=True)


def pack_body(level, noisy, obs, var, owner, cell, own, out, turned):
    count = obs.shape[2]
    slots = out.shape[0]
    noise = scale_at(level[0], (16, 256))
    inverse = 1.0 / jnp.sqrt(1.0 + noise * noise)
    for v in range(8):
        turned[:, v, :] = noisy[v] * inverse
    own[...] = turned[...].astype(BF)

    own_row = owner[...].astype(F32)
    own_col = column_of(own_row)
    row = lax.broadcasted_iota(jnp.int32, (count, count), 0)
    col = lax.broadcasted_iota(jnp.int32, (count, count), 1)
    same = (own_col == own_row) & (row < col)
    rank = jnp.sum(jnp.where(same, 1.0, 0.0), axis=0, keepdims=True)
    slot = (own_row * 8.0 + rank).astype(jnp.int32)
    near = noise[:1, :count]
    weight = 1.0 / (var[...] + near * near)
    values = jnp.concatenate([obs[k] for k in range(obs.shape[0])], axis=0) * weight
    spot = cell[...]
    extra = [weight, (spot // 256).astype(F32), (spot % 256).astype(F32)]
    spare = jnp.zeros((128 - values.shape[0] - len(extra), count), F32)
    table = jnp.concatenate([values] + extra + [spare], axis=0)
    hot = jnp.where(
        lax.broadcasted_iota(jnp.int32, (slots, count), 0) == slot, 1.0, 0.0
    ).astype(BF)
    total = None
    for part in parts_of(table):
        piece = lax.dot_general(
            hot, part, (((1,), (1,)), ((), ())), preferred_element_type=F32
        )
        total = piece if total is None else total + piece
    out[...] = total


def pack(level, noisy, obs, var, owner, cell):
    return pl.pallas_call(
        pack_body,
        out_shape=(
            jax.ShapeDtypeStruct((16, 8, 256), BF),
            jax.ShapeDtypeStruct((512, 128), F32),
        ),
        in_specs=[SM, VM, VM, VM, VM, VM],
        out_specs=(VM, VM),
        scratch_shapes=[pltpu.VMEM((16, 8, 256), F32)],
        cost_estimate=pl.CostEstimate(flops=50_000_000, bytes_accessed=400_000, transcendentals=0),
    )(level, noisy, obs, var, owner, cell)


def shifts(v):
    b = v.astype(BF)
    left, right = b[:, :256], b[:, 256:]
    return (
        jnp.concatenate([rolled(left, 1), rolled(right, 1)], 1),
        b,
        jnp.concatenate([rolled(left, -1), rolled(right, -1)], 1),
    )


def store_taps(x, row, taps):
    for k in range(3):
        at = row * 192 + k * 64
        x[at : at + 64, :] = taps[k]


def row_in(x1, row, even_t, o, a, b):
    o, a, b = o.astype(F32), a.astype(F32), b.astype(F32)
    before = jnp.where(even_t, b, a)
    later = jnp.where(even_t, a, b)
    tap_b, tap_o, tap_l = [(rolled(z, 1), z, rolled(z, -1)) for z in (before, o, later)]
    left = jnp.concatenate([z for k in range(3) for z in (tap_b[k], tap_o[k])], 0)
    right = jnp.concatenate([z for k in range(3) for z in (tap_o[k], tap_l[k])], 0)
    x1[row * 48 : (row + 1) * 48, :256] = left.astype(BF)
    x1[row * 48 : (row + 1) * 48, 256:] = right.astype(BF)


def first_rows(w1, bias, x1, x2, at, new):
    acc = jnp.dot(w1, x1[at * 48 : at * 48 + 240, :], preferred_element_type=F32)
    for r in range(3 - new, 3):
        store_taps(x2, at + r, shifts(silu_half(acc[r * 64 : (r + 1) * 64] + bias)))


def summed(weight, x, at, rows, done):
    held = []
    for y in range(rows + 2):
        piece = x[(at + y) * 192 : (at + y + 1) * 192, :]
        held.append(jnp.dot(weight, piece, preferred_element_type=F32))
        if y >= 2:
            a, b, c = held[y - 2 :]
            done(y - 2, a[128:] + b[64:128] + c[:64])


def normed(m, gain):
    mean = jnp.sum(m * m, axis=0, keepdims=True) * (1 / 64)
    return silu_half(m * lax.rsqrt(mean + 1e-05) * gain)


def store_third(x4, row, f, h):
    third = (f.astype(F32) + silu_half(h)).astype(BF)
    x4[row * 128 : row * 128 + 64, :] = third[:, :256]
    x4[row * 128 + 64 : row * 128 + 128, :] = third[:, 256:]


def out_rows(wo, x4, at, den, row):
    size = OUT_GROUP * 8
    acc = jnp.dot(wo, x4[at * 128 : (at + OUT_GROUP + 2) * 128, :], preferred_element_type=F32)
    res = rolled(acc[:size], 1) + acc[size : 2 * size] + rolled(acc[2 * size :], -1)
    for r in range(OUT_GROUP):
        den[:, row + r, :] = res[r * 8 : (r + 1) * 8]


def inner_body(
    level,
    own,
    t2,
    t1,
    conv_in,
    conv_mid,
    conv_res,
    conv_out,
    in_bias,
    noise_embed,
    norm_gain,
    w1_out,
    wm_out,
    wr_out,
    wo_out,
    columns,
    first,
    second,
    x4_edge,
    den,
    x1,
    x2,
    x3,
    x4,
):
    time_rank = lax.axis_index("tm")
    times = lax.axis_size("tm")
    even_t = time_rank % 2 == 0

    noise64 = scale_at(level[0], (1, 64))
    bias_row = 0.5 * (in_bias[...] + noise_embed[...] * jnp.log(10.0 * noise64))
    bias = column_of(bias_row)
    gain = column_of(0.5 * norm_gain[...])
    columns[0] = jnp.broadcast_to(bias, (64, 128))
    columns[1] = jnp.broadcast_to(gain, (64, 128))

    taps_in = [0.5 * conv_in[a].astype(F32).T for a in range(3)]
    spare = jnp.zeros((64, 48), F32)
    w1 = jnp.concatenate(
        [
            jnp.concatenate([taps_in[j - r] if 0 <= j - r < 3 else spare for j in range(5)], 1)
            for r in range(3)
        ],
        0,
    ).astype(BF)
    wm = jnp.concatenate([conv_mid[2], conv_mid[1], conv_mid[0]], 0)
    wr = (
        0.5 * jnp.concatenate([conv_res[2], conv_res[1], conv_res[0]], 0).astype(F32)
    ).astype(BF)
    coef0 = jnp.where(time_rank == 0, 0.0, jnp.where(time_rank == times - 1, 1.0, 0.5))
    coef1 = jnp.where(time_rank == 0, 1.0, jnp.where(time_rank == times - 1, 0.0, 0.5))
    tap_out = [conv_out[a].astype(F32) for a in range(3)]
    blank = jnp.zeros((8, 128), F32)
    banded = []
    for b in range(3):
        cell = [
            jnp.concatenate(
                [
                    coef0 * tap_out[a][8:, b * 64 : (b + 1) * 64],
                    coef1 * tap_out[a][:8, b * 64 : (b + 1) * 64],
                ],
                1,
            )
            for a in range(3)
        ]
        for r in range(OUT_GROUP):
            banded.append(
                jnp.concatenate(
                    [
                        cell[j - r] if 0 <= j - r < 3 else blank
                        for j in range(OUT_GROUP + 2)
                    ],
                    1,
                )
            )
    wo = jnp.concatenate(banded, 0).astype(BF)
    w1_out[...] = w1
    wm_out[...] = wm
    wr_out[...] = wr
    wo_out[...] = wo

    for y in range(16):
        row_in(x1, y, even_t, own[y], t1[y], t2[y])
    for at, new in ((0, 3), (3, 3), (6, 3), (9, 3), (11, 2)):
        first_rows(w1, bias, x1, x2, at, new)
    summed(wm, x2, 0, 12, lambda y, m: store_taps(x3, y, shifts(normed(m, gain))))
    summed(
        wr, x3, 0, 10, lambda y, h: store_third(x4, y, x2[(y + 2) * 192 + 64 : (y + 2) * 192 + 128, :], h)
    )
    for g in range(2):
        out_rows(wo, x4, g * 4, den, g * 4)
    for k, y in enumerate((0, 1, 12, 13)):
        first[k] = x2[y * 192 + 64 : y * 192 + 128, :]
    for k, y in enumerate((0, 1, 10, 11)):
        second[k] = x3[y * 192 + 64 : y * 192 + 128, :]
    x4_edge[:256] = x4[:256]
    x4_edge[256:] = x4[8 * 128 :]


def inner(level, *arrays):
    return pl.pallas_call(
        inner_body,
        out_shape=(
            jax.ShapeDtypeStruct((192, 240), BF),
            jax.ShapeDtypeStruct((192, 192), BF),
            jax.ShapeDtypeStruct((192, 192), BF),
            jax.ShapeDtypeStruct((96, 768), BF),
            jax.ShapeDtypeStruct((2, 64, 128), F32),
            jax.ShapeDtypeStruct((4, 64, 512), BF),
            jax.ShapeDtypeStruct((4, 64, 512), BF),
            jax.ShapeDtypeStruct((512, 256), BF),
            jax.ShapeDtypeStruct((8, 8, 256), F32),
        ),
        in_specs=[SM] + [VM] * 10,
        out_specs=(VM,) * 9,
        scratch_shapes=[
            pltpu.VMEM((16 * 48, 512), BF),
            pltpu.VMEM((14 * 192, 512), BF),
            pltpu.VMEM((12 * 192, 512), BF),
            pltpu.VMEM((10 * 128, 256), BF),
        ],
        compiler_params=pltpu.CompilerParams(vmem_limit_bytes=40 * 2**20),
        cost_estimate=pl.CostEstimate(
            flops=INNER_COST, bytes_accessed=1_000_000, transcendentals=2_000_000
        ),
    )(level, *arrays)


def outer_body(
    level,
    own,
    t2,
    t1,
    edges,
    w1,
    wm,
    wr,
    wo,
    columns,
    first,
    second,
    x4_edge,
    den_inner,
    noisy_far,
    fresh_far,
    got_far,
    out,
    x1,
    x2,
    x3,
    x4,
    den,
    noisy,
    fresh,
    got,
    sems,
):
    copies = [
        pltpu.make_async_copy(far, near, sems.at[k])
        for k, (far, near) in enumerate(((noisy_far, noisy), (fresh_far, fresh), (got_far, got)))
    ]
    for copy in copies:
        copy.start()
    even_t = lax.axis_index("tm") % 2 == 0
    even_s = lax.axis_index("space") % 2 == 0
    bias = columns[0][:, :1]
    gain = columns[1][:, :1]

    for y in range(4):
        u, v = edges[4 + y].astype(F32), edges[y].astype(F32)
        top = jnp.where(even_s, v, u)
        low = jnp.where(even_s, u, v)
        row_in(x1, y, even_t, top[16:], top[8:16], top[:8])
        row_in(x1, 8 + y, even_t, low[16:], low[8:16], low[:8])
    for y, row in ((0, 4), (1, 5), (14, 6), (15, 7)):
        row_in(x1, row, even_t, own[y], t1[y], t2[y])
    for k, row in enumerate((4, 5, 6, 7)):
        store_taps(x2, row, shifts(first[k]))
        store_taps(x3, row, shifts(second[k]))
    x4[4 * 128 : 8 * 128, :] = x4_edge[...]

    acc = [
        jnp.dot(w1[...], x1[at * 48 : at * 48 + 240, :], preferred_element_type=F32)
        for at in (0, 1, 6, 7)
    ]
    for row, k, r in (
        (0, 0, 0),
        (1, 0, 1),
        (2, 0, 2),
        (3, 1, 2),
        (8, 2, 0),
        (9, 2, 1),
        (10, 2, 2),
        (11, 3, 2),
    ):
        store_taps(x2, row, shifts(silu_half(acc[k][r * 64 : (r + 1) * 64] + bias)))

    def middle(at):
        return lambda y, m: store_taps(x3, at + y, shifts(normed(m, gain)))

    def last(at, from_first):
        def done(y, h):
            row = from_first + y
            store_third(x4, at + y, x2[row * 192 + 64 : row * 192 + 128, :], h)

        return done

    summed(wm[...], x2, 0, 4, middle(0))
    summed(wm[...], x2, 6, 4, middle(8))
    summed(wr[...], x3, 0, 4, last(0, 2))
    summed(wr[...], x3, 6, 4, last(8, 6))
    out_rows(wo[...], x4, 0, den, 0)
    den[:, 4:12, :] = den_inner[...]
    out_rows(wo[...], x4, 6, den, 12)

    for copy in copies:
        copy.wait()
    slots = got.shape[0]
    table = got[...].T
    masks = (
        lax.broadcasted_iota(jnp.int32, (16, slots), 0) == table[9:10].astype(jnp.int32)
    )
    cols = jnp.where(
        lax.broadcasted_iota(jnp.int32, (256, slots), 0) == table[10:11].astype(jnp.int32),
        1.0,
        0.0,
    ).astype(BF)
    left = jnp.concatenate(
        [jnp.where(masks, table[v : v + 1], 0.0) for v in range(9)], axis=0
    )
    total = None
    for part in parts_of(left):
        piece = lax.dot_general(
            part, cols, (((1,), (1,)), ((), ())), preferred_element_type=F32
        )
        total = piece if total is None else total + piece
    scale = scale_at(level[0], (16, 256))
    after = scale_at(level[0] - 1, (16, 256))
    square = scale * scale
    weight = 1.0 - square * total[128:144]
    for v in range(8):
        estimate = noisy[v] - scale * den[v]
        out[v] = estimate * weight + square * total[v * 16 : (v + 1) * 16] + after * fresh[v]


def outer(level, *arrays):
    return pl.pallas_call(
        outer_body,
        out_shape=jax.ShapeDtypeStruct((8, 16, 256), F32),
        in_specs=[SM] + [VM] * 13 + [ANY] * 3,
        out_specs=VM,
        scratch_shapes=[
            pltpu.VMEM((12 * 48, 512), BF),
            pltpu.VMEM((12 * 192, 512), BF),
            pltpu.VMEM((12 * 192, 512), BF),
            pltpu.VMEM((12 * 128, 256), BF),
            pltpu.VMEM((8, 16, 256), F32),
            pltpu.VMEM((8, 16, 256), F32),
            pltpu.VMEM((8, 16, 256), F32),
            pltpu.VMEM((512, 128), F32),
            pltpu.SemaphoreType.DMA((3,)),
        ],
        compiler_params=pltpu.CompilerParams(vmem_limit_bytes=40 * 2**20),
        cost_estimate=pl.CostEstimate(
            flops=4_000_000_000, bytes_accessed=1_000_000, transcendentals=1_000_000
        ),
    )(level, *arrays)


def swapped(value, axis, first):
    count = lax.axis_size(axis)
    wrap = axis == "space"
    pairs = []
    for i in range(first, count if wrap else count - 1, 2):
        j = (i + 1) % count
        pairs += [(i, j), (j, i)]
    return lax.ppermute(value, axis, pairs)


def local(
    noisy_state,
    fresh_noise,
    level_index,
    station_obs,
    obs_variance,
    station_owner,
    station_cell,
    conv_in,
    conv_mid,
    conv_res,
    conv_out,
    in_bias,
    noise_embed,
    norm_gain,
):
    even_s = lax.axis_index("space") % 2 == 0
    noisy = noisy_state.reshape(8, 16, 256)
    own, slots = pack(
        level_index,
        noisy,
        station_obs,
        obs_variance.reshape(1, 128),
        station_owner.reshape(1, 128),
        station_cell.reshape(1, 128),
    )
    t2 = swapped(own, "tm", 1)
    t1 = swapped(own, "tm", 0)
    got = lax.all_to_all(slots.reshape(64, 8, 128), "space", 0, 0, tiled=True).reshape(512, 128)

    edge = jnp.where(even_s, 12, 0)
    both = jnp.concatenate([t2, t1, own], axis=1)
    m2 = swapped(lax.dynamic_slice_in_dim(both, 12 - edge, 4, 0), "space", 1)
    m1 = swapped(lax.dynamic_slice_in_dim(both, edge, 4, 0), "space", 0)

    edges = jnp.concatenate([m2, m1], axis=0)
    held = inner(
        level_index,
        own,
        t2,
        t1,
        conv_in.transpose(0, 2, 1),
        conv_mid,
        conv_res,
        conv_out,
        in_bias.reshape(1, 64),
        noise_embed.reshape(1, 64),
        norm_gain.reshape(1, 64),
    )
    result = outer(
        level_index, own, t2, t1, edges, *held, noisy, fresh_noise.reshape(8, 16, 256), got
    )
    return result.reshape(noisy_state.shape)


def solution(mesh):
    rest = (P(),) * 7
    placed = (
        P("tm", None, "space", None),
        P("tm", None, "space", None),
        P(),
        P("tm", None, "space"),
        P("space"),
        P("space", None),
        P("space"),
    ) + rest
    return jax.shard_map(
        local, mesh=mesh, in_specs=placed, out_specs=P("tm", None, "space", None), check_vma=False
    )
```

```python
import math

import jax
import jax.numpy as jnp
from jax import lax
from jax.experimental import pallas as pl
from jax.experimental.pallas import tpu as pltpu
from jax.sharding import Mesh
from jax.sharding import PartitionSpec as P

LEVELS = 32
SPACE = ("x", "z", "core")
X_SIZE, Z_SIZE, CORES = 4, 8, 2
BF = jnp.bfloat16
F32 = jnp.float32
OUT_GROUP = 4
INNER_COST = 16_000_000_000
VM = pl.BlockSpec(memory_space=pltpu.VMEM)
SM = pl.BlockSpec(memory_space=pltpu.SMEM)
ANY = pl.BlockSpec(memory_space=pl.ANY)


def scale_at(level, shape):
    steps = jnp.full(shape, level, jnp.int32).astype(F32)
    return 0.3 * jnp.exp(math.log(5.0) * steps / (LEVELS - 1))


def rolled(x, k):
    return pltpu.roll(x, k % x.shape[1], 1)


def parts_of(v):
    high = v.astype(BF)
    rest = v - high.astype(F32)
    middle = rest.astype(BF)
    low = (rest - middle.astype(F32)).astype(BF)
    return high, middle, low


def silu_half(h):
    return h + h * jnp.tanh(h)


def column_of(row):
    size = row.shape[1]
    line = lax.broadcasted_iota(jnp.int32, (size, size), 0)
    lane = lax.broadcasted_iota(jnp.int32, (size, size), 1)
    return jnp.sum(jnp.where(line == lane, row, 0.0), axis=1, keepdims=True)


def pack_body(level, noisy, obs, var, owner, cell, own, out, turned):
    count = obs.shape[2]
    slots = out.shape[0]
    noise = scale_at(level[0], (16, 256))
    inverse = 1.0 / jnp.sqrt(1.0 + noise * noise)
    for v in range(8):
        turned[:, v, :] = noisy[v] * inverse
    own[...] = turned[...].astype(BF)

    own_row = owner[...].astype(F32)
    own_col = column_of(own_row)
    row = lax.broadcasted_iota(jnp.int32, (count, count), 0)
    col = lax.broadcasted_iota(jnp.int32, (count, count), 1)
    same = (own_col == own_row) & (row < col)
    rank = jnp.sum(jnp.where(same, 1.0, 0.0), axis=0, keepdims=True)
    strip = owner[...]
    x_core = (strip // (Z_SIZE * CORES)) * CORES + strip % CORES
    block = x_core * Z_SIZE + (strip // CORES) % Z_SIZE
    slot = block * 8 + rank.astype(jnp.int32)
    near = noise[:1, :count]
    weight = 1.0 / (var[...] + near * near)
    values = jnp.concatenate([obs[k] for k in range(obs.shape[0])], axis=0) * weight
    spot = cell[...]
    extra = [weight, (spot // 256).astype(F32), (spot % 256).astype(F32)]
    spare = jnp.zeros((128 - values.shape[0] - len(extra), count), F32)
    table = jnp.concatenate([values] + extra + [spare], axis=0)
    hot = jnp.where(
        lax.broadcasted_iota(jnp.int32, (slots, count), 0) == slot, 1.0, 0.0
    ).astype(BF)
    total = None
    for part in parts_of(table):
        piece = lax.dot_general(
            hot, part, (((1,), (1,)), ((), ())), preferred_element_type=F32
        )
        total = piece if total is None else total + piece
    out[...] = total


def pack(level, noisy, obs, var, owner, cell):
    return pl.pallas_call(
        pack_body,
        out_shape=(
            jax.ShapeDtypeStruct((16, 8, 256), BF),
            jax.ShapeDtypeStruct((512, 128), F32),
        ),
        in_specs=[SM, VM, VM, VM, VM, VM],
        out_specs=(VM, VM),
        scratch_shapes=[pltpu.VMEM((16, 8, 256), F32)],
        cost_estimate=pl.CostEstimate(flops=50_000_000, bytes_accessed=400_000, transcendentals=0),
    )(level, noisy, obs, var, owner, cell)


def shifts(v):
    b = v.astype(BF)
    left, right = b[:, :256], b[:, 256:]
    return (
        jnp.concatenate([rolled(left, 1), rolled(right, 1)], 1),
        b,
        jnp.concatenate([rolled(left, -1), rolled(right, -1)], 1),
    )


def store_taps(x, row, taps):
    for k in range(3):
        at = row * 192 + k * 64
        x[at : at + 64, :] = taps[k]


def row_in(x1, row, even_t, o, a, b):
    o, a, b = o.astype(F32), a.astype(F32), b.astype(F32)
    before = jnp.where(even_t, b, a)
    later = jnp.where(even_t, a, b)
    tap_b, tap_o, tap_l = [(rolled(z, 1), z, rolled(z, -1)) for z in (before, o, later)]
    left = jnp.concatenate([z for k in range(3) for z in (tap_b[k], tap_o[k])], 0)
    right = jnp.concatenate([z for k in range(3) for z in (tap_o[k], tap_l[k])], 0)
    x1[row * 48 : (row + 1) * 48, :256] = left.astype(BF)
    x1[row * 48 : (row + 1) * 48, 256:] = right.astype(BF)


def first_rows(w1, bias, x1, x2, at, new):
    acc = jnp.dot(w1, x1[at * 48 : at * 48 + 240, :], preferred_element_type=F32)
    for r in range(3 - new, 3):
        store_taps(x2, at + r, shifts(silu_half(acc[r * 64 : (r + 1) * 64] + bias)))


def summed(weight, x, at, rows, done):
    held = []
    for y in range(rows + 2):
        piece = x[(at + y) * 192 : (at + y + 1) * 192, :]
        held.append(jnp.dot(weight, piece, preferred_element_type=F32))
        if y >= 2:
            a, b, c = held[y - 2 :]
            done(y - 2, a[128:] + b[64:128] + c[:64])


def normed(m, gain):
    mean = jnp.sum(m * m, axis=0, keepdims=True) * (1 / 64)
    return silu_half(m * lax.rsqrt(mean + 1e-05) * gain)


def store_third(x4, row, f, h):
    third = (f.astype(F32) + silu_half(h)).astype(BF)
    x4[row * 128 : row * 128 + 64, :] = third[:, :256]
    x4[row * 128 + 64 : row * 128 + 128, :] = third[:, 256:]


def out_rows(wo, x4, at, den, row):
    size = OUT_GROUP * 8
    acc = jnp.dot(wo, x4[at * 128 : (at + OUT_GROUP + 2) * 128, :], preferred_element_type=F32)
    res = rolled(acc[:size], 1) + acc[size : 2 * size] + rolled(acc[2 * size :], -1)
    for r in range(OUT_GROUP):
        den[:, row + r, :] = res[r * 8 : (r + 1) * 8]


def inner_body(
    level,
    own,
    t2,
    t1,
    conv_in,
    conv_mid,
    conv_res,
    conv_out,
    in_bias,
    noise_embed,
    norm_gain,
    w1_out,
    wm_out,
    wr_out,
    wo_out,
    columns,
    first,
    second,
    x4_edge,
    den,
    x1,
    x2,
    x3,
    x4,
):
    time_rank = lax.axis_index("tm")
    times = lax.axis_size("tm")
    even_t = time_rank % 2 == 0

    noise64 = scale_at(level[0], (1, 64))
    bias_row = 0.5 * (in_bias[...] + noise_embed[...] * jnp.log(10.0 * noise64))
    bias = column_of(bias_row)
    gain = column_of(0.5 * norm_gain[...])
    columns[0] = jnp.broadcast_to(bias, (64, 128))
    columns[1] = jnp.broadcast_to(gain, (64, 128))

    taps_in = [0.5 * conv_in[a].astype(F32).T for a in range(3)]
    spare = jnp.zeros((64, 48), F32)
    w1 = jnp.concatenate(
        [
            jnp.concatenate([taps_in[j - r] if 0 <= j - r < 3 else spare for j in range(5)], 1)
            for r in range(3)
        ],
        0,
    ).astype(BF)
    wm = jnp.concatenate([conv_mid[2], conv_mid[1], conv_mid[0]], 0)
    wr = (
        0.5 * jnp.concatenate([conv_res[2], conv_res[1], conv_res[0]], 0).astype(F32)
    ).astype(BF)
    coef0 = jnp.where(time_rank == 0, 0.0, jnp.where(time_rank == times - 1, 1.0, 0.5))
    coef1 = jnp.where(time_rank == 0, 1.0, jnp.where(time_rank == times - 1, 0.0, 0.5))
    tap_out = [conv_out[a].astype(F32) for a in range(3)]
    blank = jnp.zeros((8, 128), F32)
    banded = []
    for b in range(3):
        cell = [
            jnp.concatenate(
                [
                    coef0 * tap_out[a][8:, b * 64 : (b + 1) * 64],
                    coef1 * tap_out[a][:8, b * 64 : (b + 1) * 64],
                ],
                1,
            )
            for a in range(3)
        ]
        for r in range(OUT_GROUP):
            banded.append(
                jnp.concatenate(
                    [
                        cell[j - r] if 0 <= j - r < 3 else blank
                        for j in range(OUT_GROUP + 2)
                    ],
                    1,
                )
            )
    wo = jnp.concatenate(banded, 0).astype(BF)
    w1_out[...] = w1
    wm_out[...] = wm
    wr_out[...] = wr
    wo_out[...] = wo

    for y in range(16):
        row_in(x1, y, even_t, own[y], t1[y], t2[y])
    for at, new in ((0, 3), (3, 3), (6, 3), (9, 3), (11, 2)):
        first_rows(w1, bias, x1, x2, at, new)
    summed(wm, x2, 0, 12, lambda y, m: store_taps(x3, y, shifts(normed(m, gain))))
    summed(
        wr, x3, 0, 10, lambda y, h: store_third(x4, y, x2[(y + 2) * 192 + 64 : (y + 2) * 192 + 128, :], h)
    )
    for g in range(2):
        out_rows(wo, x4, g * 4, den, g * 4)
    for k, y in enumerate((0, 1, 12, 13)):
        first[k] = x2[y * 192 + 64 : y * 192 + 128, :]
    for k, y in enumerate((0, 1, 10, 11)):
        second[k] = x3[y * 192 + 64 : y * 192 + 128, :]
    x4_edge[:256] = x4[:256]
    x4_edge[256:] = x4[8 * 128 :]


def inner(level, *arrays):
    return pl.pallas_call(
        inner_body,
        out_shape=(
            jax.ShapeDtypeStruct((192, 240), BF),
            jax.ShapeDtypeStruct((192, 192), BF),
            jax.ShapeDtypeStruct((192, 192), BF),
            jax.ShapeDtypeStruct((96, 768), BF),
            jax.ShapeDtypeStruct((2, 64, 128), F32),
            jax.ShapeDtypeStruct((4, 64, 512), BF),
            jax.ShapeDtypeStruct((4, 64, 512), BF),
            jax.ShapeDtypeStruct((512, 256), BF),
            jax.ShapeDtypeStruct((8, 8, 256), F32),
        ),
        in_specs=[SM] + [VM] * 10,
        out_specs=(VM,) * 9,
        scratch_shapes=[
            pltpu.VMEM((16 * 48, 512), BF),
            pltpu.VMEM((14 * 192, 512), BF),
            pltpu.VMEM((12 * 192, 512), BF),
            pltpu.VMEM((10 * 128, 256), BF),
        ],
        compiler_params=pltpu.CompilerParams(vmem_limit_bytes=40 * 2**20),
        cost_estimate=pl.CostEstimate(
            flops=INNER_COST, bytes_accessed=1_000_000, transcendentals=2_000_000
        ),
    )(level, *arrays)


def outer_body(
    level,
    own,
    t2,
    t1,
    edges,
    w1,
    wm,
    wr,
    wo,
    columns,
    first,
    second,
    x4_edge,
    den_inner,
    noisy_far,
    fresh_far,
    got_far,
    out,
    x1,
    x2,
    x3,
    x4,
    den,
    noisy,
    fresh,
    got,
    sems,
):
    copies = [
        pltpu.make_async_copy(far, near, sems.at[k])
        for k, (far, near) in enumerate(((noisy_far, noisy), (fresh_far, fresh), (got_far, got)))
    ]
    for copy in copies:
        copy.start()
    even_t = lax.axis_index("tm") % 2 == 0
    even_s = lax.axis_index(SPACE) % 2 == 0
    bias = columns[0][:, :1]
    gain = columns[1][:, :1]

    for y in range(4):
        u, v = edges[4 + y].astype(F32), edges[y].astype(F32)
        top = jnp.where(even_s, v, u)
        low = jnp.where(even_s, u, v)
        row_in(x1, y, even_t, top[16:], top[8:16], top[:8])
        row_in(x1, 8 + y, even_t, low[16:], low[8:16], low[:8])
    for y, row in ((0, 4), (1, 5), (14, 6), (15, 7)):
        row_in(x1, row, even_t, own[y], t1[y], t2[y])
    for k, row in enumerate((4, 5, 6, 7)):
        store_taps(x2, row, shifts(first[k]))
        store_taps(x3, row, shifts(second[k]))
    x4[4 * 128 : 8 * 128, :] = x4_edge[...]

    acc = [
        jnp.dot(w1[...], x1[at * 48 : at * 48 + 240, :], preferred_element_type=F32)
        for at in (0, 1, 6, 7)
    ]
    for row, k, r in (
        (0, 0, 0),
        (1, 0, 1),
        (2, 0, 2),
        (3, 1, 2),
        (8, 2, 0),
        (9, 2, 1),
        (10, 2, 2),
        (11, 3, 2),
    ):
        store_taps(x2, row, shifts(silu_half(acc[k][r * 64 : (r + 1) * 64] + bias)))

    def middle(at):
        return lambda y, m: store_taps(x3, at + y, shifts(normed(m, gain)))

    def last(at, from_first):
        def done(y, h):
            row = from_first + y
            store_third(x4, at + y, x2[row * 192 + 64 : row * 192 + 128, :], h)

        return done

    summed(wm[...], x2, 0, 4, middle(0))
    summed(wm[...], x2, 6, 4, middle(8))
    summed(wr[...], x3, 0, 4, last(0, 2))
    summed(wr[...], x3, 6, 4, last(8, 6))
    out_rows(wo[...], x4, 0, den, 0)
    den[:, 4:12, :] = den_inner[...]
    out_rows(wo[...], x4, 6, den, 12)

    for copy in copies:
        copy.wait()
    slots = got.shape[0]
    table = got[...].T
    masks = (
        lax.broadcasted_iota(jnp.int32, (16, slots), 0) == table[9:10].astype(jnp.int32)
    )
    cols = jnp.where(
        lax.broadcasted_iota(jnp.int32, (256, slots), 0) == table[10:11].astype(jnp.int32),
        1.0,
        0.0,
    ).astype(BF)
    left = jnp.concatenate(
        [jnp.where(masks, table[v : v + 1], 0.0) for v in range(9)], axis=0
    )
    total = None
    for part in parts_of(left):
        piece = lax.dot_general(
            part, cols, (((1,), (1,)), ((), ())), preferred_element_type=F32
        )
        total = piece if total is None else total + piece
    scale = scale_at(level[0], (16, 256))
    after = scale_at(level[0] - 1, (16, 256))
    square = scale * scale
    weight = 1.0 - square * total[128:144]
    for v in range(8):
        estimate = noisy[v] - scale * den[v]
        out[v] = estimate * weight + square * total[v * 16 : (v + 1) * 16] + after * fresh[v]


def outer(level, *arrays):
    return pl.pallas_call(
        outer_body,
        out_shape=jax.ShapeDtypeStruct((8, 16, 256), F32),
        in_specs=[SM] + [VM] * 13 + [ANY] * 3,
        out_specs=VM,
        scratch_shapes=[
            pltpu.VMEM((12 * 48, 512), BF),
            pltpu.VMEM((12 * 192, 512), BF),
            pltpu.VMEM((12 * 192, 512), BF),
            pltpu.VMEM((12 * 128, 256), BF),
            pltpu.VMEM((8, 16, 256), F32),
            pltpu.VMEM((8, 16, 256), F32),
            pltpu.VMEM((8, 16, 256), F32),
            pltpu.VMEM((512, 128), F32),
            pltpu.SemaphoreType.DMA((3,)),
        ],
        compiler_params=pltpu.CompilerParams(vmem_limit_bytes=40 * 2**20),
        cost_estimate=pl.CostEstimate(
            flops=4_000_000_000, bytes_accessed=1_000_000, transcendentals=1_000_000
        ),
    )(level, *arrays)


def swapped(value, axis, first):
    count = lax.axis_size(axis)
    wrap = axis == SPACE
    pairs = []
    for i in range(first, count if wrap else count - 1, 2):
        j = (i + 1) % count
        pairs += [(i, j), (j, i)]
    return lax.ppermute(value, axis, pairs)


def local(
    noisy_state,
    fresh_noise,
    level_index,
    station_obs,
    obs_variance,
    station_owner,
    station_cell,
    conv_in,
    conv_mid,
    conv_res,
    conv_out,
    in_bias,
    noise_embed,
    norm_gain,
):
    even_s = lax.axis_index(SPACE) % 2 == 0
    noisy = noisy_state.reshape(8, 16, 256)
    own, slots = pack(
        level_index,
        noisy,
        station_obs,
        obs_variance.reshape(1, 128),
        station_owner.reshape(1, 128),
        station_cell.reshape(1, 128),
    )
    t2 = swapped(own, "tm", 1)
    t1 = swapped(own, "tm", 0)
    near = lax.all_to_all(slots.reshape(8, 8, 8, 128), ("x", "core"), 0, 0, tiled=True)
    near = near.transpose(1, 0, 2, 3)
    got = lax.all_to_all(near, "z", 0, 0, tiled=True).reshape(512, 128)

    edge = jnp.where(even_s, 12, 0)
    both = jnp.concatenate([t2, t1, own], axis=1)
    m2 = swapped(lax.dynamic_slice_in_dim(both, 12 - edge, 4, 0), SPACE, 1)
    m1 = swapped(lax.dynamic_slice_in_dim(both, edge, 4, 0), SPACE, 0)

    edges = jnp.concatenate([m2, m1], axis=0)
    held = inner(
        level_index,
        own,
        t2,
        t1,
        conv_in.transpose(0, 2, 1),
        conv_mid,
        conv_res,
        conv_out,
        in_bias.reshape(1, 64),
        noise_embed.reshape(1, 64),
        norm_gain.reshape(1, 64),
    )
    result = outer(
        level_index, own, t2, t1, edges, *held, noisy, fresh_noise.reshape(8, 16, 256), got
    )
    return result.reshape(noisy_state.shape)


def solution(mesh):
    times = mesh.shape["tm"]
    fine = Mesh(mesh.devices.reshape(times, X_SIZE, Z_SIZE, CORES), ("tm",) + SPACE)
    rest = (P(),) * 7
    placed = (
        P("tm", None, SPACE, None),
        P("tm", None, SPACE, None),
        P(),
        P("tm", None, SPACE),
        P(SPACE),
        P(SPACE, None),
        P(SPACE),
    ) + rest
    return jax.shard_map(
        local, mesh=fine, in_specs=placed, out_specs=P("tm", None, SPACE, None), check_vma=False
    )
```

```python
import math

import jax
import jax.numpy as jnp
from jax import lax
from jax.experimental import pallas as pl
from jax.experimental.pallas import tpu as pltpu
from jax.sharding import PartitionSpec as P

LEVELS = 32
LEADER = 8
BF = jnp.bfloat16
F32 = jnp.float32
OUT_GROUP = 4
INNER_COST = 8_000_000_000
VM = pl.BlockSpec(memory_space=pltpu.VMEM)
SM = pl.BlockSpec(memory_space=pltpu.SMEM)
ANY = pl.BlockSpec(memory_space=pl.ANY)


def scale_at(level, shape):
    steps = jnp.full(shape, level, jnp.int32).astype(F32)
    return 0.3 * jnp.exp(math.log(5.0) * steps / (LEVELS - 1))


def rolled(x, k):
    return pltpu.roll(x, k % x.shape[1], 1)


def parts_of(v):
    high = v.astype(BF)
    rest = v - high.astype(F32)
    middle = rest.astype(BF)
    low = (rest - middle.astype(F32)).astype(BF)
    return high, middle, low


def silu_half(h):
    return h + h * jnp.tanh(h)


def column_of(row):
    size = row.shape[1]
    line = lax.broadcasted_iota(jnp.int32, (size, size), 0)
    lane = lax.broadcasted_iota(jnp.int32, (size, size), 1)
    return jnp.sum(jnp.where(line == lane, row, 0.0), axis=1, keepdims=True)


def pack_body(level, noisy, obs, var, owner, cell, own, out, turned):
    count = obs.shape[2]
    peers = out.shape[0]
    noise = scale_at(level[0], (16, 256))
    inverse = 1.0 / jnp.sqrt(1.0 + noise * noise)
    for v in range(8):
        turned[:, v, :] = noisy[v] * inverse
    own[...] = turned[...].astype(BF)

    strip = owner[...]
    own_row = strip.astype(F32)
    own_col = column_of(own_row)
    row = lax.broadcasted_iota(jnp.int32, (count, count), 0)
    col = lax.broadcasted_iota(jnp.int32, (count, count), 1)
    same = (own_col == own_row) & (row < col)
    rank = jnp.sum(jnp.where(same, 1.0, 0.0), axis=0, keepdims=True)
    near = noise[:1, :count]
    weight = 1.0 / (var[...] + near * near)
    values = jnp.concatenate([obs[k] for k in range(obs.shape[0])], axis=0) * weight
    spot = cell[...]
    extra = [weight, (spot // 256).astype(F32), (spot % 256).astype(F32)]
    spare = jnp.zeros((16 - values.shape[0] - len(extra), count), F32)
    table = jnp.concatenate([values] + extra + [spare], axis=0)
    ranked = jnp.concatenate([jnp.where(rank == float(k), table, 0.0) for k in range(8)], axis=0)
    hot = jnp.where(
        lax.broadcasted_iota(jnp.int32, (peers, count), 0) == (strip + (peers - LEADER)) % peers, 1.0, 0.0
    ).astype(BF)
    total = None
    for part in parts_of(ranked):
        piece = lax.dot_general(
            hot, part, (((1,), (1,)), ((), ())), preferred_element_type=F32
        )
        total = piece if total is None else total + piece
    out[:, 0, :] = total


def pack(level, noisy, obs, var, owner, cell):
    return pl.pallas_call(
        pack_body,
        out_shape=(
            jax.ShapeDtypeStruct((16, 8, 256), BF),
            jax.ShapeDtypeStruct((64, 1, 128), F32),
        ),
        in_specs=[SM, VM, VM, VM, VM, VM],
        out_specs=(VM, VM),
        scratch_shapes=[pltpu.VMEM((16, 8, 256), F32)],
        cost_estimate=pl.CostEstimate(flops=50_000_000, bytes_accessed=400_000, transcendentals=0),
    )(level, noisy, obs, var, owner, cell)


def shifts(v):
    b = v.astype(BF)
    left, right = b[:, :256], b[:, 256:]
    return (
        jnp.concatenate([rolled(left, 1), rolled(right, 1)], 1),
        b,
        jnp.concatenate([rolled(left, -1), rolled(right, -1)], 1),
    )


def store_taps(x, row, taps):
    for k in range(3):
        at = row * 192 + k * 64
        x[at : at + 64, :] = taps[k]


def row_in(x1, row, even_t, o, a, b):
    o, a, b = o.astype(F32), a.astype(F32), b.astype(F32)
    before = jnp.where(even_t, b, a)
    later = jnp.where(even_t, a, b)
    tap_b, tap_o, tap_l = [(rolled(z, 1), z, rolled(z, -1)) for z in (before, o, later)]
    left = jnp.concatenate([z for k in range(3) for z in (tap_b[k], tap_o[k])], 0)
    right = jnp.concatenate([z for k in range(3) for z in (tap_o[k], tap_l[k])], 0)
    x1[row * 48 : (row + 1) * 48, :256] = left.astype(BF)
    x1[row * 48 : (row + 1) * 48, 256:] = right.astype(BF)


def first_rows(w1, bias, x1, x2, at, new):
    acc = jnp.dot(w1, x1[at * 48 : at * 48 + 240, :], preferred_element_type=F32)
    for r in range(3 - new, 3):
        store_taps(x2, at + r, shifts(silu_half(acc[r * 64 : (r + 1) * 64] + bias)))


def summed(weight, x, at, rows, done):
    held = []
    for y in range(rows + 2):
        piece = x[(at + y) * 192 : (at + y + 1) * 192, :]
        held.append(jnp.dot(weight, piece, preferred_element_type=F32))
        if y >= 2:
            a, b, c = held[y - 2 :]
            done(y - 2, a[128:] + b[64:128] + c[:64])


def normed(m, gain):
    mean = jnp.sum(m * m, axis=0, keepdims=True) * (1 / 64)
    return silu_half(m * lax.rsqrt(mean + 1e-05) * gain)


def store_third(x4, row, f, h):
    third = (f.astype(F32) + silu_half(h)).astype(BF)
    x4[row * 128 : row * 128 + 64, :] = third[:, :256]
    x4[row * 128 + 64 : row * 128 + 128, :] = third[:, 256:]


def out_rows(wo, x4, at, den, row):
    size = OUT_GROUP * 8
    acc = jnp.dot(wo, x4[at * 128 : (at + OUT_GROUP + 2) * 128, :], preferred_element_type=F32)
    res = rolled(acc[:size], 1) + acc[size : 2 * size] + rolled(acc[2 * size :], -1)
    for r in range(OUT_GROUP):
        den[:, row + r, :] = res[r * 8 : (r + 1) * 8]


def inner_body(
    level,
    own,
    t2,
    t1,
    conv_in,
    conv_mid,
    conv_res,
    conv_out,
    in_bias,
    noise_embed,
    norm_gain,
    w1_out,
    wm_out,
    wr_out,
    wo_out,
    columns,
    first,
    second,
    x4_edge,
    den,
    x1,
    x2,
    x3,
    x4,
):
    time_rank = lax.axis_index("tm")
    times = lax.axis_size("tm")
    even_t = time_rank % 2 == 0

    noise64 = scale_at(level[0], (1, 64))
    bias_row = 0.5 * (in_bias[...] + noise_embed[...] * jnp.log(10.0 * noise64))
    bias = column_of(bias_row)
    gain = column_of(0.5 * norm_gain[...])
    columns[0] = jnp.broadcast_to(bias, (64, 128))
    columns[1] = jnp.broadcast_to(gain, (64, 128))

    taps_in = [0.5 * conv_in[a].astype(F32).T for a in range(3)]
    spare = jnp.zeros((64, 48), F32)
    w1 = jnp.concatenate(
        [
            jnp.concatenate([taps_in[j - r] if 0 <= j - r < 3 else spare for j in range(5)], 1)
            for r in range(3)
        ],
        0,
    ).astype(BF)
    wm = jnp.concatenate([conv_mid[2], conv_mid[1], conv_mid[0]], 0)
    wr = (
        0.5 * jnp.concatenate([conv_res[2], conv_res[1], conv_res[0]], 0).astype(F32)
    ).astype(BF)
    coef0 = jnp.where(time_rank == 0, 0.0, jnp.where(time_rank == times - 1, 1.0, 0.5))
    coef1 = jnp.where(time_rank == 0, 1.0, jnp.where(time_rank == times - 1, 0.0, 0.5))
    tap_out = [conv_out[a].astype(F32) for a in range(3)]
    blank = jnp.zeros((8, 128), F32)
    banded = []
    for b in range(3):
        cell = [
            jnp.concatenate(
                [
                    coef0 * tap_out[a][8:, b * 64 : (b + 1) * 64],
                    coef1 * tap_out[a][:8, b * 64 : (b + 1) * 64],
                ],
                1,
            )
            for a in range(3)
        ]
        for r in range(OUT_GROUP):
            banded.append(
                jnp.concatenate(
                    [
                        cell[j - r] if 0 <= j - r < 3 else blank
                        for j in range(OUT_GROUP + 2)
                    ],
                    1,
                )
            )
    wo = jnp.concatenate(banded, 0).astype(BF)
    w1_out[...] = w1
    wm_out[...] = wm
    wr_out[...] = wr
    wo_out[...] = wo

    for y in range(16):
        row_in(x1, y, even_t, own[y], t1[y], t2[y])
    for at, new in ((0, 3), (3, 3), (6, 3), (9, 3), (11, 2)):
        first_rows(w1, bias, x1, x2, at, new)
    summed(wm, x2, 0, 12, lambda y, m: store_taps(x3, y, shifts(normed(m, gain))))
    summed(
        wr, x3, 0, 10, lambda y, h: store_third(x4, y, x2[(y + 2) * 192 + 64 : (y + 2) * 192 + 128, :], h)
    )
    for g in range(2):
        out_rows(wo, x4, g * 4, den, g * 4)
    for k, y in enumerate((0, 1, 12, 13)):
        first[k] = x2[y * 192 + 64 : y * 192 + 128, :]
    for k, y in enumerate((0, 1, 10, 11)):
        second[k] = x3[y * 192 + 64 : y * 192 + 128, :]
    x4_edge[:256] = x4[:256]
    x4_edge[256:] = x4[8 * 128 :]


def inner(level, *arrays):
    return pl.pallas_call(
        inner_body,
        out_shape=(
            jax.ShapeDtypeStruct((192, 240), BF),
            jax.ShapeDtypeStruct((192, 192), BF),
            jax.ShapeDtypeStruct((192, 192), BF),
            jax.ShapeDtypeStruct((96, 768), BF),
            jax.ShapeDtypeStruct((2, 64, 128), F32),
            jax.ShapeDtypeStruct((4, 64, 512), BF),
            jax.ShapeDtypeStruct((4, 64, 512), BF),
            jax.ShapeDtypeStruct((512, 256), BF),
            jax.ShapeDtypeStruct((8, 8, 256), F32),
        ),
        in_specs=[SM] + [VM] * 10,
        out_specs=(VM,) * 9,
        scratch_shapes=[
            pltpu.VMEM((16 * 48, 512), BF),
            pltpu.VMEM((14 * 192, 512), BF),
            pltpu.VMEM((12 * 192, 512), BF),
            pltpu.VMEM((10 * 128, 256), BF),
        ],
        compiler_params=pltpu.CompilerParams(vmem_limit_bytes=40 * 2**20),
        cost_estimate=pl.CostEstimate(
            flops=INNER_COST, bytes_accessed=1_000_000, transcendentals=2_000_000
        ),
    )(level, *arrays)


def outer_body(
    level,
    own,
    t2,
    t1,
    edges,
    w1,
    wm,
    wr,
    wo,
    columns,
    first,
    second,
    x4_edge,
    den_inner,
    noisy_far,
    fresh_far,
    got_far,
    out,
    x1,
    x2,
    x3,
    x4,
    den,
    noisy,
    fresh,
    got,
    sems,
):
    copies = [
        pltpu.make_async_copy(far, near, sems.at[k])
        for k, (far, near) in enumerate(((noisy_far, noisy), (fresh_far, fresh), (got_far, got)))
    ]
    for copy in copies:
        copy.start()
    even_t = lax.axis_index("tm") % 2 == 0
    even_s = lax.axis_index("space") % 2 == 0
    bias = columns[0][:, :1]
    gain = columns[1][:, :1]

    for y in range(4):
        u, v = edges[4 + y].astype(F32), edges[y].astype(F32)
        top = jnp.where(even_s, v, u)
        low = jnp.where(even_s, u, v)
        row_in(x1, y, even_t, top[16:], top[8:16], top[:8])
        row_in(x1, 8 + y, even_t, low[16:], low[8:16], low[:8])
    for y, row in ((0, 4), (1, 5), (14, 6), (15, 7)):
        row_in(x1, row, even_t, own[y], t1[y], t2[y])
    for k, row in enumerate((4, 5, 6, 7)):
        store_taps(x2, row, shifts(first[k]))
        store_taps(x3, row, shifts(second[k]))
    x4[4 * 128 : 8 * 128, :] = x4_edge[...]

    acc = [
        jnp.dot(w1[...], x1[at * 48 : at * 48 + 240, :], preferred_element_type=F32)
        for at in (0, 1, 6, 7)
    ]
    for row, k, r in (
        (0, 0, 0),
        (1, 0, 1),
        (2, 0, 2),
        (3, 1, 2),
        (8, 2, 0),
        (9, 2, 1),
        (10, 2, 2),
        (11, 3, 2),
    ):
        store_taps(x2, row, shifts(silu_half(acc[k][r * 64 : (r + 1) * 64] + bias)))

    def middle(at):
        return lambda y, m: store_taps(x3, at + y, shifts(normed(m, gain)))

    def last(at, from_first):
        def done(y, h):
            row = from_first + y
            store_third(x4, at + y, x2[row * 192 + 64 : row * 192 + 128, :], h)

        return done

    summed(wm[...], x2, 0, 4, middle(0))
    summed(wm[...], x2, 6, 4, middle(8))
    summed(wr[...], x3, 0, 4, last(0, 2))
    summed(wr[...], x3, 6, 4, last(8, 6))
    out_rows(wo[...], x4, 0, den, 0)
    den[:, 4:12, :] = den_inner[...]
    out_rows(wo[...], x4, 6, den, 12)

    for copy in copies:
        copy.wait()
    wide = got[:, 0, :].T
    table = jnp.concatenate([wide[k * 16 : (k + 1) * 16] for k in range(8)], axis=1)
    slots = table.shape[1]
    masks = (
        lax.broadcasted_iota(jnp.int32, (16, slots), 0) == table[9:10].astype(jnp.int32)
    )
    cols = jnp.where(
        lax.broadcasted_iota(jnp.int32, (256, slots), 0) == table[10:11].astype(jnp.int32),
        1.0,
        0.0,
    ).astype(BF)
    left = jnp.concatenate(
        [jnp.where(masks, table[v : v + 1], 0.0) for v in range(9)], axis=0
    )
    total = None
    for part in parts_of(left):
        piece = lax.dot_general(
            part, cols, (((1,), (1,)), ((), ())), preferred_element_type=F32
        )
        total = piece if total is None else total + piece
    scale = scale_at(level[0], (16, 256))
    after = scale_at(level[0] - 1, (16, 256))
    square = scale * scale
    weight = 1.0 - square * total[128:144]
    for v in range(8):
        estimate = noisy[v] - scale * den[v]
        out[v] = estimate * weight + square * total[v * 16 : (v + 1) * 16] + after * fresh[v]


def outer(level, *arrays):
    return pl.pallas_call(
        outer_body,
        out_shape=jax.ShapeDtypeStruct((8, 16, 256), F32),
        in_specs=[SM] + [VM] * 13 + [ANY] * 3,
        out_specs=VM,
        scratch_shapes=[
            pltpu.VMEM((12 * 48, 512), BF),
            pltpu.VMEM((12 * 192, 512), BF),
            pltpu.VMEM((12 * 192, 512), BF),
            pltpu.VMEM((12 * 128, 256), BF),
            pltpu.VMEM((8, 16, 256), F32),
            pltpu.VMEM((8, 16, 256), F32),
            pltpu.VMEM((8, 16, 256), F32),
            pltpu.VMEM((64, 1, 128), F32),
            pltpu.SemaphoreType.DMA((3,)),
        ],
        compiler_params=pltpu.CompilerParams(vmem_limit_bytes=40 * 2**20),
        cost_estimate=pl.CostEstimate(
            flops=4_000_000_000, bytes_accessed=1_000_000, transcendentals=1_000_000
        ),
    )(level, *arrays)


def order_of(count):
    return [(k + LEADER) % count for k in range(count)]


def swapped(value, axis, first):
    count = lax.axis_size(axis)
    wrap = axis == "space"
    pairs = []
    for i in range(first, count if wrap else count - 1, 2):
        j = (i + 1) % count
        pairs += [(i, j), (j, i)]
    return lax.ppermute(value, axis, pairs)


def local(
    noisy_state,
    fresh_noise,
    level_index,
    station_obs,
    obs_variance,
    station_owner,
    station_cell,
    conv_in,
    conv_mid,
    conv_res,
    conv_out,
    in_bias,
    noise_embed,
    norm_gain,
):
    even_s = lax.axis_index("space") % 2 == 0
    noisy = noisy_state.reshape(8, 16, 256)
    own, slots = pack(
        level_index,
        noisy,
        station_obs,
        obs_variance.reshape(1, 128),
        station_owner.reshape(1, 128),
        station_cell.reshape(1, 128),
    )
    t2 = swapped(own, "tm", 1)
    t1 = swapped(own, "tm", 0)
    got = lax.all_to_all(
        slots, "space", 0, 0, axis_index_groups=[order_of(slots.shape[0])], tiled=True
    )

    edge = jnp.where(even_s, 12, 0)
    both = jnp.concatenate([t2, t1, own], axis=1)
    m2 = swapped(lax.dynamic_slice_in_dim(both, 12 - edge, 4, 0), "space", 1)
    m1 = swapped(lax.dynamic_slice_in_dim(both, edge, 4, 0), "space", 0)

    edges = jnp.concatenate([m2, m1], axis=0)
    held = inner(
        level_index,
        own,
        t2,
        t1,
        conv_in.transpose(0, 2, 1),
        conv_mid,
        conv_res,
        conv_out,
        in_bias.reshape(1, 64),
        noise_embed.reshape(1, 64),
        norm_gain.reshape(1, 64),
    )
    result = outer(
        level_index, own, t2, t1, edges, *held, noisy, fresh_noise.reshape(8, 16, 256), got
    )
    return result.reshape(noisy_state.shape)


def solution(mesh):
    rest = (P(),) * 7
    placed = (
        P("tm", None, "space", None),
        P("tm", None, "space", None),
        P(),
        P("tm", None, "space"),
        P("space"),
        P("space", None),
        P("space"),
    ) + rest
    return jax.shard_map(
        local, mesh=mesh, in_specs=placed, out_specs=P("tm", None, "space", None), check_vma=False
    )
```

```python
import math

import jax
import jax.numpy as jnp
from jax import lax
from jax.experimental import pallas as pl
from jax.experimental.pallas import tpu as pltpu
from jax.sharding import PartitionSpec as P

LEVELS = 32
LEADER = 8
BF = jnp.bfloat16
F32 = jnp.float32
OUT_GROUP = 4
INNER_COST = 8_000_000_000
VM = pl.BlockSpec(memory_space=pltpu.VMEM)
SM = pl.BlockSpec(memory_space=pltpu.SMEM)
ANY = pl.BlockSpec(memory_space=pl.ANY)


def scale_at(level, shape):
    steps = jnp.full(shape, level, jnp.int32).astype(F32)
    return 0.3 * jnp.exp(math.log(5.0) * steps / (LEVELS - 1))


def rolled(x, k):
    return pltpu.roll(x, k % x.shape[1], 1)


def parts_of(v):
    high = v.astype(BF)
    rest = v - high.astype(F32)
    middle = rest.astype(BF)
    low = (rest - middle.astype(F32)).astype(BF)
    return high, middle, low


def silu_half(h):
    return h + h * jnp.tanh(h)


def column_of(row):
    size = row.shape[1]
    line = lax.broadcasted_iota(jnp.int32, (size, size), 0)
    lane = lax.broadcasted_iota(jnp.int32, (size, size), 1)
    return jnp.sum(jnp.where(line == lane, row, 0.0), axis=1, keepdims=True)


def pack_body(level, noisy, obs, var, owner, cell, own, out, turned):
    count = obs.shape[2]
    peers = out.shape[0]
    noise = scale_at(level[0], (16, 256))
    inverse = 1.0 / jnp.sqrt(1.0 + noise * noise)
    for v in range(8):
        turned[:, v, :] = noisy[v] * inverse
    own[...] = turned[...].astype(BF)

    strip = owner[...]
    own_row = strip.astype(F32)
    own_col = column_of(own_row)
    row = lax.broadcasted_iota(jnp.int32, (count, count), 0)
    col = lax.broadcasted_iota(jnp.int32, (count, count), 1)
    same = (own_col == own_row) & (row < col)
    rank = jnp.sum(jnp.where(same, 1.0, 0.0), axis=0, keepdims=True)
    near = noise[:1, :count]
    weight = 1.0 / (var[...] + near * near)
    values = jnp.concatenate([obs[k] for k in range(obs.shape[0])], axis=0) * weight
    spot = cell[...]
    extra = [weight, (spot // 256).astype(F32), (spot % 256).astype(F32)]
    spare = jnp.zeros((16 - values.shape[0] - len(extra), count), F32)
    table = jnp.concatenate([values] + extra + [spare], axis=0)
    ranked = jnp.concatenate([jnp.where(rank == float(k), table, 0.0) for k in range(8)], axis=0)
    hot = jnp.where(
        lax.broadcasted_iota(jnp.int32, (peers, count), 0) == (strip + (peers - LEADER)) % peers, 1.0, 0.0
    ).astype(BF)
    total = None
    for part in parts_of(ranked):
        piece = lax.dot_general(
            hot, part, (((1,), (1,)), ((), ())), preferred_element_type=F32
        )
        total = piece if total is None else total + piece
    out[:, 0, :] = total


def pack(level, noisy, obs, var, owner, cell):
    return pl.pallas_call(
        pack_body,
        out_shape=(
            jax.ShapeDtypeStruct((16, 8, 256), BF),
            jax.ShapeDtypeStruct((64, 1, 128), F32),
        ),
        in_specs=[SM, VM, VM, VM, VM, VM],
        out_specs=(VM, VM),
        scratch_shapes=[pltpu.VMEM((16, 8, 256), F32)],
        cost_estimate=pl.CostEstimate(flops=50_000_000, bytes_accessed=400_000, transcendentals=0),
    )(level, noisy, obs, var, owner, cell)


def shifts(v):
    b = v.astype(BF)
    left, right = b[:, :256], b[:, 256:]
    return (
        jnp.concatenate([rolled(left, 1), rolled(right, 1)], 1),
        b,
        jnp.concatenate([rolled(left, -1), rolled(right, -1)], 1),
    )


def store_taps(x, row, taps):
    for k in range(3):
        at = row * 192 + k * 64
        x[at : at + 64, :] = taps[k]


def row_in(x1, row, even_t, o, a, b):
    o, a, b = o.astype(F32), a.astype(F32), b.astype(F32)
    before = jnp.where(even_t, b, a)
    later = jnp.where(even_t, a, b)
    tap_b, tap_o, tap_l = [(rolled(z, 1), z, rolled(z, -1)) for z in (before, o, later)]
    left = jnp.concatenate([z for k in range(3) for z in (tap_b[k], tap_o[k])], 0)
    right = jnp.concatenate([z for k in range(3) for z in (tap_o[k], tap_l[k])], 0)
    x1[row * 48 : (row + 1) * 48, :256] = left.astype(BF)
    x1[row * 48 : (row + 1) * 48, 256:] = right.astype(BF)


def first_rows(w1, bias, x1, x2, at, new):
    acc = jnp.dot(w1, x1[at * 48 : at * 48 + 240, :], preferred_element_type=F32)
    for r in range(3 - new, 3):
        store_taps(x2, at + r, shifts(silu_half(acc[r * 64 : (r + 1) * 64] + bias)))


def pieces_of(*sources):
    return [ref.at[(at + k) * 192 : (at + k + 1) * 192] for ref, at, rows in sources for k in range(rows)]


def summed(weight, pieces, done):
    held = []
    for y, piece in enumerate(pieces):
        held.append(jnp.dot(weight, piece[...], preferred_element_type=F32))
        if y >= 2:
            a, b, c = held[y - 2 :]
            done(y - 2, a[128:] + b[64:128] + c[:64])


def normed(m, gain):
    mean = jnp.sum(m * m, axis=0, keepdims=True) * (1 / 64)
    return silu_half(m * lax.rsqrt(mean + 1e-05) * gain)


def store_third(x4, row, f, h):
    third = (f.astype(F32) + silu_half(h)).astype(BF)
    x4[row * 128 : row * 128 + 64, :] = third[:, :256]
    x4[row * 128 + 64 : row * 128 + 128, :] = third[:, 256:]


def out_rows(wo, x4, at, den, row):
    size = OUT_GROUP * 8
    acc = jnp.dot(wo, x4[at * 128 : (at + OUT_GROUP + 2) * 128, :], preferred_element_type=F32)
    res = rolled(acc[:size], 1) + acc[size : 2 * size] + rolled(acc[2 * size :], -1)
    for r in range(OUT_GROUP):
        den[:, row + r, :] = res[r * 8 : (r + 1) * 8]


def station_sums(got):
    wide = got[:, 0, :].T
    table = jnp.concatenate([wide[k * 16 : (k + 1) * 16] for k in range(8)], axis=1)
    slots = table.shape[1]
    masks = (
        lax.broadcasted_iota(jnp.int32, (16, slots), 0) == table[9:10].astype(jnp.int32)
    )
    cols = jnp.where(
        lax.broadcasted_iota(jnp.int32, (256, slots), 0) == table[10:11].astype(jnp.int32),
        1.0,
        0.0,
    ).astype(BF)
    left = jnp.concatenate(
        [jnp.where(masks, table[v : v + 1], 0.0) for v in range(9)], axis=0
    )
    total = None
    for part in parts_of(left):
        piece = lax.dot_general(
            part, cols, (((1,), (1,)), ((), ())), preferred_element_type=F32
        )
        total = piece if total is None else total + piece
    return total


def inner_body(
    level,
    own,
    t1,
    t2,
    conv_in,
    conv_mid,
    conv_res,
    conv_out,
    in_bias,
    noise_embed,
    norm_gain,
    w1_out,
    wm_out,
    wr_out,
    wo_out,
    columns,
    x1_edge,
    x2_edge,
    x3_edge,
    x4_edge,
    den,
    x1,
    x2,
    x3,
    x4,
):
    time_rank = lax.axis_index("tm")
    times = lax.axis_size("tm")
    even_t = time_rank % 2 == 0

    noise64 = scale_at(level[0], (1, 64))
    bias_row = 0.5 * (in_bias[...] + noise_embed[...] * jnp.log(10.0 * noise64))
    bias = column_of(bias_row)
    gain = column_of(0.5 * norm_gain[...])
    columns[0] = jnp.broadcast_to(bias, (64, 128))
    columns[1] = jnp.broadcast_to(gain, (64, 128))

    taps_in = [0.5 * conv_in[a].astype(F32).T for a in range(3)]
    spare = jnp.zeros((64, 48), F32)
    w1 = jnp.concatenate(
        [
            jnp.concatenate([taps_in[j - r] if 0 <= j - r < 3 else spare for j in range(5)], 1)
            for r in range(3)
        ],
        0,
    ).astype(BF)
    wm = jnp.concatenate([conv_mid[2], conv_mid[1], conv_mid[0]], 0)
    wr = (
        0.5 * jnp.concatenate([conv_res[2], conv_res[1], conv_res[0]], 0).astype(F32)
    ).astype(BF)
    coef0 = jnp.where(time_rank == 0, 0.0, jnp.where(time_rank == times - 1, 1.0, 0.5))
    coef1 = jnp.where(time_rank == 0, 1.0, jnp.where(time_rank == times - 1, 0.0, 0.5))
    tap_out = [conv_out[a].astype(F32) for a in range(3)]
    blank = jnp.zeros((8, 128), F32)
    banded = []
    for b in range(3):
        cell = [
            jnp.concatenate(
                [
                    coef0 * tap_out[a][8:, b * 64 : (b + 1) * 64],
                    coef1 * tap_out[a][:8, b * 64 : (b + 1) * 64],
                ],
                1,
            )
            for a in range(3)
        ]
        for r in range(OUT_GROUP):
            banded.append(
                jnp.concatenate(
                    [
                        cell[j - r] if 0 <= j - r < 3 else blank
                        for j in range(OUT_GROUP + 2)
                    ],
                    1,
                )
            )
    wo = jnp.concatenate(banded, 0).astype(BF)
    w1_out[...] = w1
    wm_out[...] = wm
    wr_out[...] = wr
    wo_out[...] = wo

    for y in range(16):
        row_in(x1, y, even_t, own[y], t1[y], t2[y])
    for at, new in ((0, 3), (3, 3), (6, 3), (9, 3), (11, 2)):
        first_rows(w1, bias, x1, x2, at, new)
    summed(wm, pieces_of((x2, 0, 14)), lambda y, m: store_taps(x3, y, shifts(normed(m, gain))))

    def last(y, h):
        store_third(x4, y, x2[(y + 2) * 192 + 64 : (y + 2) * 192 + 128, :], h)

    summed(wr, pieces_of((x3, 0, 12)), last)
    for g in range(2):
        out_rows(wo, x4, g * 4, den, g * 4)
    x1_edge[:96] = x1[:96]
    x1_edge[96:] = x1[14 * 48 :]
    x2_edge[:384] = x2[:384]
    x2_edge[384:] = x2[12 * 192 :]
    x3_edge[:384] = x3[:384]
    x3_edge[384:] = x3[10 * 192 :]
    x4_edge[:256] = x4[:256]
    x4_edge[256:] = x4[8 * 128 :]


def inner(level, *arrays):
    return pl.pallas_call(
        inner_body,
        out_shape=(
            jax.ShapeDtypeStruct((192, 240), BF),
            jax.ShapeDtypeStruct((192, 192), BF),
            jax.ShapeDtypeStruct((192, 192), BF),
            jax.ShapeDtypeStruct((96, 768), BF),
            jax.ShapeDtypeStruct((2, 64, 128), F32),
            jax.ShapeDtypeStruct((4 * 48, 512), BF),
            jax.ShapeDtypeStruct((4 * 192, 512), BF),
            jax.ShapeDtypeStruct((4 * 192, 512), BF),
            jax.ShapeDtypeStruct((512, 256), BF),
            jax.ShapeDtypeStruct((8, 8, 256), F32),
        ),
        in_specs=[SM] + [VM] * 10,
        out_specs=(VM,) * 10,
        scratch_shapes=[
            pltpu.VMEM((16 * 48, 512), BF),
            pltpu.VMEM((14 * 192, 512), BF),
            pltpu.VMEM((12 * 192, 512), BF),
            pltpu.VMEM((10 * 128, 256), BF),
        ],
        compiler_params=pltpu.CompilerParams(vmem_limit_bytes=40 * 2**20),
        cost_estimate=pl.CostEstimate(
            flops=INNER_COST, bytes_accessed=1_000_000, transcendentals=2_000_000
        ),
    )(level, *arrays)


def outer_body(
    level,
    edges,
    w1,
    wm,
    wr,
    wo,
    columns,
    x1_edge,
    x2_edge,
    x3_edge,
    x4_edge,
    den_inner,
    got,
    noisy_far,
    fresh_far,
    out,
    x1,
    x2,
    x3,
    x4,
    den,
    noisy,
    fresh,
    sems,
):
    copies = [
        pltpu.make_async_copy(far, near, sems.at[k])
        for k, (far, near) in enumerate(((noisy_far, noisy), (fresh_far, fresh)))
    ]
    for copy in copies:
        copy.start()
    even_t = lax.axis_index("tm") % 2 == 0
    even_s = lax.axis_index("space") % 2 == 0
    total = station_sums(got)
    bias = columns[0][:, :1]
    gain = columns[1][:, :1]

    for y in range(4):
        u, v = edges[4 + y].astype(F32), edges[y].astype(F32)
        top = jnp.where(even_s, v, u)
        low = jnp.where(even_s, u, v)
        row_in(x1, y, even_t, top[:8], top[16:], top[8:16])
        row_in(x1, 8 + y, even_t, low[:8], low[16:], low[8:16])
    x1[4 * 48 : 8 * 48, :] = x1_edge[...]
    x4[4 * 128 : 8 * 128, :] = x4_edge[...]

    acc = [
        jnp.dot(w1[...], x1[at * 48 : at * 48 + 240, :], preferred_element_type=F32)
        for at in (0, 1, 6, 7)
    ]
    for row, k, r in (
        (0, 0, 0),
        (1, 0, 1),
        (2, 0, 2),
        (3, 1, 2),
        (4, 2, 0),
        (5, 2, 1),
        (6, 2, 2),
        (7, 3, 2),
    ):
        store_taps(x2, row, shifts(silu_half(acc[k][r * 64 : (r + 1) * 64] + bias)))

    def middle(at):
        return lambda y, m: store_taps(x3, at + y, shifts(normed(m, gain)))

    def last(at, ref, from_first, more):
        def done(y, h):
            source, row = (ref, from_first + y) if y < 2 else (more, y - 2)
            store_third(x4, at + y, source[row * 192 + 64 : row * 192 + 128, :], h)

        return done

    summed(wm[...], pieces_of((x2, 0, 4), (x2_edge, 0, 2)), middle(0))
    summed(wm[...], pieces_of((x2_edge, 2, 2), (x2, 4, 4)), middle(4))
    summed(wr[...], pieces_of((x3, 0, 4), (x3_edge, 0, 2)), last(0, x2, 2, x2_edge))
    summed(wr[...], pieces_of((x3_edge, 2, 2), (x3, 4, 4)), last(8, x2_edge, 2, x2.at[4 * 192 :]))
    out_rows(wo[...], x4, 0, den, 0)
    den[:, 4:12, :] = den_inner[...]
    out_rows(wo[...], x4, 6, den, 12)

    for copy in copies:
        copy.wait()
    scale = scale_at(level[0], (16, 256))
    after = scale_at(level[0] - 1, (16, 256))
    square = scale * scale
    weight = 1.0 - square * total[128:144]
    for v in range(8):
        estimate = noisy[v] - scale * den[v]
        out[v] = estimate * weight + square * total[v * 16 : (v + 1) * 16] + after * fresh[v]


def outer(level, *arrays):
    return pl.pallas_call(
        outer_body,
        out_shape=jax.ShapeDtypeStruct((8, 16, 256), F32),
        in_specs=[SM] + [VM] * 12 + [ANY] * 2,
        out_specs=VM,
        scratch_shapes=[
            pltpu.VMEM((12 * 48, 512), BF),
            pltpu.VMEM((8 * 192, 512), BF),
            pltpu.VMEM((8 * 192, 512), BF),
            pltpu.VMEM((12 * 128, 256), BF),
            pltpu.VMEM((8, 16, 256), F32),
            pltpu.VMEM((8, 16, 256), F32),
            pltpu.VMEM((8, 16, 256), F32),
            pltpu.SemaphoreType.DMA((2,)),
        ],
        compiler_params=pltpu.CompilerParams(vmem_limit_bytes=40 * 2**20),
        cost_estimate=pl.CostEstimate(
            flops=4_000_000_000, bytes_accessed=1_000_000, transcendentals=1_000_000
        ),
    )(level, *arrays)


def order_of(count):
    return [(k + LEADER) % count for k in range(count)]


def swapped(value, axis, first):
    count = lax.axis_size(axis)
    wrap = axis == "space"
    pairs = []
    for i in range(first, count if wrap else count - 1, 2):
        j = (i + 1) % count
        pairs += [(i, j), (j, i)]
    return lax.ppermute(value, axis, pairs)


def local(
    noisy_state,
    fresh_noise,
    level_index,
    station_obs,
    obs_variance,
    station_owner,
    station_cell,
    conv_in,
    conv_mid,
    conv_res,
    conv_out,
    in_bias,
    noise_embed,
    norm_gain,
):
    even_s = lax.axis_index("space") % 2 == 0
    noisy = noisy_state.reshape(8, 16, 256)
    own, slots = pack(
        level_index,
        noisy,
        station_obs,
        obs_variance.reshape(1, 128),
        station_owner.reshape(1, 128),
        station_cell.reshape(1, 128),
    )
    t1 = swapped(own, "tm", 0)
    t2 = swapped(own, "tm", 1)
    got = lax.all_to_all(
        slots, "space", 0, 0, axis_index_groups=[order_of(slots.shape[0])], tiled=True
    )

    edge = jnp.where(even_s, 12, 0)
    both = jnp.concatenate([own, t2, t1], axis=1)
    m2 = swapped(lax.dynamic_slice_in_dim(both, 12 - edge, 4, 0), "space", 1)
    m1 = swapped(lax.dynamic_slice_in_dim(both, edge, 4, 0), "space", 0)

    edges = jnp.concatenate([m2, m1], axis=0)
    held = inner(
        level_index,
        own,
        t1,
        t2,
        conv_in.transpose(0, 2, 1),
        conv_mid,
        conv_res,
        conv_out,
        in_bias.reshape(1, 64),
        noise_embed.reshape(1, 64),
        norm_gain.reshape(1, 64),
    )
    result = outer(
        level_index, edges, *held, got, noisy, fresh_noise.reshape(8, 16, 256)
    )
    return result.reshape(noisy_state.shape)


def solution(mesh):
    rest = (P(),) * 7
    placed = (
        P("tm", None, "space", None),
        P("tm", None, "space", None),
        P(),
        P("tm", None, "space"),
        P("space"),
        P("space", None),
        P("space"),
    ) + rest
    return jax.shard_map(
        local, mesh=mesh, in_specs=placed, out_specs=P("tm", None, "space", None), check_vma=False
    )
```

```python
import math

import jax
import jax.numpy as jnp
from jax import lax
from jax.experimental import pallas as pl
from jax.experimental.pallas import tpu as pltpu
from jax.sharding import PartitionSpec as P

LEVELS = 32
LEADER = 8
BF = jnp.bfloat16
F32 = jnp.float32
OUT_GROUP = 4
STATION_COST = 400_000_000
INNER_COST = 8_000_000_000
VM = pl.BlockSpec(memory_space=pltpu.VMEM)
SM = pl.BlockSpec(memory_space=pltpu.SMEM)


def scale_at(level, shape):
    steps = jnp.full(shape, level, jnp.int32).astype(F32)
    return 0.3 * jnp.exp(math.log(5.0) * steps / (LEVELS - 1))


def rolled(x, k):
    return pltpu.roll(x, k % x.shape[1], 1)


def parts_of(v):
    high = v.astype(BF)
    rest = v - high.astype(F32)
    middle = rest.astype(BF)
    low = (rest - middle.astype(F32)).astype(BF)
    return high, middle, low


def silu_half(h):
    return h + h * jnp.tanh(h)


def column_of(row):
    size = row.shape[1]
    line = lax.broadcasted_iota(jnp.int32, (size, size), 0)
    lane = lax.broadcasted_iota(jnp.int32, (size, size), 1)
    return jnp.sum(jnp.where(line == lane, row, 0.0), axis=1, keepdims=True)


def pack_body(level, noisy, obs, var, owner, cell, own, out, turned):
    count = obs.shape[2]
    peers = out.shape[0]
    noise = scale_at(level[0], (16, 256))
    inverse = 1.0 / jnp.sqrt(1.0 + noise * noise)
    for v in range(8):
        turned[:, v, :] = noisy[v] * inverse
    own[...] = turned[...].astype(BF)

    strip = owner[...]
    own_row = strip.astype(F32)
    own_col = column_of(own_row)
    row = lax.broadcasted_iota(jnp.int32, (count, count), 0)
    col = lax.broadcasted_iota(jnp.int32, (count, count), 1)
    same = (own_col == own_row) & (row < col)
    rank = jnp.sum(jnp.where(same, 1.0, 0.0), axis=0, keepdims=True)
    near = noise[:1, :count]
    weight = 1.0 / (var[...] + near * near)
    values = jnp.concatenate([obs[k] for k in range(obs.shape[0])], axis=0) * weight
    spot = cell[...]
    extra = [weight, (spot // 256).astype(F32), (spot % 256).astype(F32)]
    spare = jnp.zeros((16 - values.shape[0] - len(extra), count), F32)
    table = jnp.concatenate([values] + extra + [spare], axis=0)
    ranked = jnp.concatenate([jnp.where(rank == float(k), table, 0.0) for k in range(8)], axis=0)
    hot = jnp.where(
        lax.broadcasted_iota(jnp.int32, (peers, count), 0) == (strip + (peers - LEADER)) % peers, 1.0, 0.0
    ).astype(BF)
    total = None
    for part in parts_of(ranked):
        piece = lax.dot_general(
            hot, part, (((1,), (1,)), ((), ())), preferred_element_type=F32
        )
        total = piece if total is None else total + piece
    out[:, 0, :] = total


def pack(level, noisy, obs, var, owner, cell):
    return pl.pallas_call(
        pack_body,
        out_shape=(
            jax.ShapeDtypeStruct((16, 8, 256), BF),
            jax.ShapeDtypeStruct((64, 1, 128), F32),
        ),
        in_specs=[SM, VM, VM, VM, VM, VM],
        out_specs=(VM, VM),
        scratch_shapes=[pltpu.VMEM((16, 8, 256), F32)],
        cost_estimate=pl.CostEstimate(flops=50_000_000, bytes_accessed=400_000, transcendentals=0),
    )(level, noisy, obs, var, owner, cell)


def shifts(v):
    b = v.astype(BF)
    left, right = b[:, :256], b[:, 256:]
    return (
        jnp.concatenate([rolled(left, 1), rolled(right, 1)], 1),
        b,
        jnp.concatenate([rolled(left, -1), rolled(right, -1)], 1),
    )


def store_taps(x, row, taps):
    for k in range(3):
        at = row * 192 + k * 64
        x[at : at + 64, :] = taps[k]


def row_in(x1, row, even_t, o, a, b):
    o, a, b = o.astype(F32), a.astype(F32), b.astype(F32)
    before = jnp.where(even_t, b, a)
    later = jnp.where(even_t, a, b)
    tap_b, tap_o, tap_l = [(rolled(z, 1), z, rolled(z, -1)) for z in (before, o, later)]
    left = jnp.concatenate([z for k in range(3) for z in (tap_b[k], tap_o[k])], 0)
    right = jnp.concatenate([z for k in range(3) for z in (tap_o[k], tap_l[k])], 0)
    x1[row * 48 : (row + 1) * 48, :256] = left.astype(BF)
    x1[row * 48 : (row + 1) * 48, 256:] = right.astype(BF)


def first_rows(w1, bias, x1, x2, at, new):
    acc = jnp.dot(w1, x1[at * 48 : at * 48 + 240, :], preferred_element_type=F32)
    for r in range(3 - new, 3):
        store_taps(x2, at + r, shifts(silu_half(acc[r * 64 : (r + 1) * 64] + bias)))


def pieces_of(*sources):
    return [ref.at[(at + k) * 192 : (at + k + 1) * 192] for ref, at, rows in sources for k in range(rows)]


def summed(weight, pieces, done):
    held = []
    for y, piece in enumerate(pieces):
        held.append(jnp.dot(weight, piece[...], preferred_element_type=F32))
        if y >= 2:
            a, b, c = held[y - 2 :]
            done(y - 2, a[128:] + b[64:128] + c[:64])


def normed(m, gain):
    mean = jnp.sum(m * m, axis=0, keepdims=True) * (1 / 64)
    return silu_half(m * lax.rsqrt(mean + 1e-05) * gain)


def store_third(x4, row, f, h):
    third = (f.astype(F32) + silu_half(h)).astype(BF)
    x4[row * 128 : row * 128 + 64, :] = third[:, :256]
    x4[row * 128 + 64 : row * 128 + 128, :] = third[:, 256:]


def out_rows(wo, x4, at, den, row):
    size = OUT_GROUP * 8
    acc = jnp.dot(wo, x4[at * 128 : (at + OUT_GROUP + 2) * 128, :], preferred_element_type=F32)
    res = rolled(acc[:size], 1) + acc[size : 2 * size] + rolled(acc[2 * size :], -1)
    for r in range(OUT_GROUP):
        den[:, row + r, :] = res[r * 8 : (r + 1) * 8]


def station_body(level, noisy, fresh, got, base, slope):
    wide = got[:, 0, :].T
    table = jnp.concatenate([wide[k * 16 : (k + 1) * 16] for k in range(8)], axis=1)
    slots = table.shape[1]
    masks = (
        lax.broadcasted_iota(jnp.int32, (16, slots), 0) == table[9:10].astype(jnp.int32)
    )
    cols = jnp.where(
        lax.broadcasted_iota(jnp.int32, (256, slots), 0) == table[10:11].astype(jnp.int32),
        1.0,
        0.0,
    ).astype(BF)
    left = jnp.concatenate(
        [jnp.where(masks, table[v : v + 1], 0.0) for v in range(9)], axis=0
    )
    total = None
    for part in parts_of(left):
        piece = lax.dot_general(
            part, cols, (((1,), (1,)), ((), ())), preferred_element_type=F32
        )
        total = piece if total is None else total + piece
    scale = scale_at(level[0], (16, 256))
    after = scale_at(level[0] - 1, (16, 256))
    square = scale * scale
    weight = 1.0 - square * total[128:144]
    slope[...] = scale * weight
    for v in range(8):
        base[v] = noisy[v] * weight + square * total[v * 16 : (v + 1) * 16] + after * fresh[v]


def station_terms(level, noisy, fresh, got):
    return pl.pallas_call(
        station_body,
        out_shape=(
            jax.ShapeDtypeStruct((8, 16, 256), F32),
            jax.ShapeDtypeStruct((16, 256), F32),
        ),
        in_specs=[SM, VM, VM, VM],
        out_specs=(VM, VM),
        cost_estimate=pl.CostEstimate(
            flops=STATION_COST, bytes_accessed=400_000, transcendentals=0
        ),
    )(level, noisy, fresh, got)


def inner_body(
    level,
    own,
    low,
    t2,
    high,
    conv_in,
    conv_mid,
    conv_res,
    conv_out,
    in_bias,
    noise_embed,
    norm_gain,
    w1_out,
    wm_out,
    wr_out,
    wo_out,
    columns,
    x1_edge,
    x2_edge,
    x3_edge,
    x4_edge,
    den,
    x1,
    x2,
    x3,
    x4,
):
    time_rank = lax.axis_index("tm")
    times = lax.axis_size("tm")
    even_t = time_rank % 2 == 0
    lower = time_rank < times // 2

    noise64 = scale_at(level[0], (1, 64))
    bias_row = 0.5 * (in_bias[...] + noise_embed[...] * jnp.log(10.0 * noise64))
    bias = column_of(bias_row)
    gain = column_of(0.5 * norm_gain[...])
    columns[0] = jnp.broadcast_to(bias, (64, 128))
    columns[1] = jnp.broadcast_to(gain, (64, 128))

    taps_in = [0.5 * conv_in[a].astype(F32).T for a in range(3)]
    spare = jnp.zeros((64, 48), F32)
    w1 = jnp.concatenate(
        [
            jnp.concatenate([taps_in[j - r] if 0 <= j - r < 3 else spare for j in range(5)], 1)
            for r in range(3)
        ],
        0,
    ).astype(BF)
    wm = jnp.concatenate([conv_mid[2], conv_mid[1], conv_mid[0]], 0)
    wr = (
        0.5 * jnp.concatenate([conv_res[2], conv_res[1], conv_res[0]], 0).astype(F32)
    ).astype(BF)
    coef0 = jnp.where(time_rank == 0, 0.0, jnp.where(time_rank == times - 1, 1.0, 0.5))
    coef1 = jnp.where(time_rank == 0, 1.0, jnp.where(time_rank == times - 1, 0.0, 0.5))
    tap_out = [conv_out[a].astype(F32) for a in range(3)]
    blank = jnp.zeros((8, 128), F32)
    banded = []
    for b in range(3):
        cell = [
            jnp.concatenate(
                [
                    coef0 * tap_out[a][8:, b * 64 : (b + 1) * 64],
                    coef1 * tap_out[a][:8, b * 64 : (b + 1) * 64],
                ],
                1,
            )
            for a in range(3)
        ]
        for r in range(OUT_GROUP):
            banded.append(
                jnp.concatenate(
                    [
                        cell[j - r] if 0 <= j - r < 3 else blank
                        for j in range(OUT_GROUP + 2)
                    ],
                    1,
                )
            )
    wo = jnp.concatenate(banded, 0).astype(BF)
    w1_out[...] = w1
    wm_out[...] = wm
    wr_out[...] = wr
    wo_out[...] = wo

    for y in range(16):
        row_in(x1, y, even_t, own[y], jnp.where(lower, low[y], high[y]), t2[y])
    for at, new in ((0, 3), (3, 3), (6, 3), (9, 3), (11, 2)):
        first_rows(w1, bias, x1, x2, at, new)
    summed(wm, pieces_of((x2, 0, 14)), lambda y, m: store_taps(x3, y, shifts(normed(m, gain))))

    def last(y, h):
        store_third(x4, y, x2[(y + 2) * 192 + 64 : (y + 2) * 192 + 128, :], h)

    summed(wr, pieces_of((x3, 0, 12)), last)
    for g in range(2):
        out_rows(wo, x4, g * 4, den, g * 4)
    x1_edge[:96] = x1[:96]
    x1_edge[96:] = x1[14 * 48 :]
    x2_edge[:384] = x2[:384]
    x2_edge[384:] = x2[12 * 192 :]
    x3_edge[:384] = x3[:384]
    x3_edge[384:] = x3[10 * 192 :]
    x4_edge[:256] = x4[:256]
    x4_edge[256:] = x4[8 * 128 :]


def inner(level, *arrays):
    return pl.pallas_call(
        inner_body,
        out_shape=(
            jax.ShapeDtypeStruct((192, 240), BF),
            jax.ShapeDtypeStruct((192, 192), BF),
            jax.ShapeDtypeStruct((192, 192), BF),
            jax.ShapeDtypeStruct((96, 768), BF),
            jax.ShapeDtypeStruct((2, 64, 128), F32),
            jax.ShapeDtypeStruct((4 * 48, 512), BF),
            jax.ShapeDtypeStruct((4 * 192, 512), BF),
            jax.ShapeDtypeStruct((4 * 192, 512), BF),
            jax.ShapeDtypeStruct((512, 256), BF),
            jax.ShapeDtypeStruct((8, 8, 256), F32),
        ),
        in_specs=[SM] + [VM] * 11,
        out_specs=(VM,) * 10,
        scratch_shapes=[
            pltpu.VMEM((16 * 48, 512), BF),
            pltpu.VMEM((14 * 192, 512), BF),
            pltpu.VMEM((12 * 192, 512), BF),
            pltpu.VMEM((10 * 128, 256), BF),
        ],
        compiler_params=pltpu.CompilerParams(vmem_limit_bytes=40 * 2**20),
        cost_estimate=pl.CostEstimate(
            flops=INNER_COST, bytes_accessed=1_000_000, transcendentals=2_000_000
        ),
    )(level, *arrays)


def outer_body(
    edges,
    w1,
    wm,
    wr,
    wo,
    columns,
    x1_edge,
    x2_edge,
    x3_edge,
    x4_edge,
    den_inner,
    base,
    slope,
    out,
    x1,
    x2,
    x3,
    x4,
    den,
):
    time_rank = lax.axis_index("tm")
    even_t = time_rank % 2 == 0
    lower = time_rank < lax.axis_size("tm") // 2
    even_s = lax.axis_index("space") % 2 == 0
    bias = columns[0][:, :1]
    gain = columns[1][:, :1]

    for y in range(4):
        u, v = edges[4 + y].astype(F32), edges[y].astype(F32)
        top = jnp.where(even_s, v, u)
        low = jnp.where(even_s, u, v)
        row_in(x1, y, even_t, top[:8], jnp.where(lower, top[8:16], top[24:]), top[16:24])
        row_in(x1, 8 + y, even_t, low[:8], jnp.where(lower, low[8:16], low[24:]), low[16:24])
    x1[4 * 48 : 8 * 48, :] = x1_edge[...]
    x4[4 * 128 : 8 * 128, :] = x4_edge[...]

    acc = [
        jnp.dot(w1[...], x1[at * 48 : at * 48 + 240, :], preferred_element_type=F32)
        for at in (0, 1, 6, 7)
    ]
    for row, k, r in (
        (0, 0, 0),
        (1, 0, 1),
        (2, 0, 2),
        (3, 1, 2),
        (4, 2, 0),
        (5, 2, 1),
        (6, 2, 2),
        (7, 3, 2),
    ):
        store_taps(x2, row, shifts(silu_half(acc[k][r * 64 : (r + 1) * 64] + bias)))

    def middle(at):
        return lambda y, m: store_taps(x3, at + y, shifts(normed(m, gain)))

    def last(at, ref, from_first, more):
        def done(y, h):
            source, row = (ref, from_first + y) if y < 2 else (more, y - 2)
            store_third(x4, at + y, source[row * 192 + 64 : row * 192 + 128, :], h)

        return done

    summed(wm[...], pieces_of((x2, 0, 4), (x2_edge, 0, 2)), middle(0))
    summed(wm[...], pieces_of((x2_edge, 2, 2), (x2, 4, 4)), middle(4))
    summed(wr[...], pieces_of((x3, 0, 4), (x3_edge, 0, 2)), last(0, x2, 2, x2_edge))
    summed(wr[...], pieces_of((x3_edge, 2, 2), (x3, 4, 4)), last(8, x2_edge, 2, x2.at[4 * 192 :]))
    out_rows(wo[...], x4, 0, den, 0)
    den[:, 4:12, :] = den_inner[...]
    out_rows(wo[...], x4, 6, den, 12)

    for v in range(8):
        out[v] = base[v] - slope[...] * den[v]


def outer(*arrays):
    return pl.pallas_call(
        outer_body,
        out_shape=jax.ShapeDtypeStruct((8, 16, 256), F32),
        in_specs=[VM] * 13,
        out_specs=VM,
        scratch_shapes=[
            pltpu.VMEM((12 * 48, 512), BF),
            pltpu.VMEM((8 * 192, 512), BF),
            pltpu.VMEM((8 * 192, 512), BF),
            pltpu.VMEM((12 * 128, 256), BF),
            pltpu.VMEM((8, 16, 256), F32),
        ],
        compiler_params=pltpu.CompilerParams(vmem_limit_bytes=40 * 2**20),
        cost_estimate=pl.CostEstimate(
            flops=4_000_000_000, bytes_accessed=1_000_000, transcendentals=1_000_000
        ),
    )(*arrays)


def order_of(count):
    return [(k + LEADER) % count for k in range(count)]


def swapped(value, axis, first, stop=None):
    count = lax.axis_size(axis)
    wrap = axis == "space"
    pairs = []
    for i in range(first, count if wrap else stop or count - 1, 2):
        j = (i + 1) % count
        pairs += [(i, j), (j, i)]
    return lax.ppermute(value, axis, pairs)


def local(
    noisy_state,
    fresh_noise,
    level_index,
    station_obs,
    obs_variance,
    station_owner,
    station_cell,
    conv_in,
    conv_mid,
    conv_res,
    conv_out,
    in_bias,
    noise_embed,
    norm_gain,
):
    even_s = lax.axis_index("space") % 2 == 0
    noisy = noisy_state.reshape(8, 16, 256)
    own, slots = pack(
        level_index,
        noisy,
        station_obs,
        obs_variance.reshape(1, 128),
        station_owner.reshape(1, 128),
        station_cell.reshape(1, 128),
    )
    half = lax.axis_size("tm") // 2
    low = swapped(own, "tm", 0, half)
    t2 = swapped(own, "tm", 1)
    high = swapped(own, "tm", half)
    got = lax.all_to_all(
        slots, "space", 0, 0, axis_index_groups=[order_of(slots.shape[0])], tiled=True
    )

    edge = jnp.where(even_s, 12, 0)
    both = jnp.concatenate([own, low, t2, high], axis=1)
    m2 = swapped(lax.dynamic_slice_in_dim(both, 12 - edge, 4, 0), "space", 1)
    m1 = swapped(lax.dynamic_slice_in_dim(both, edge, 4, 0), "space", 0)

    edges = jnp.concatenate([m2, m1], axis=0)
    held = inner(
        level_index,
        own,
        low,
        t2,
        high,
        conv_in.transpose(0, 2, 1),
        conv_mid,
        conv_res,
        conv_out,
        in_bias.reshape(1, 64),
        noise_embed.reshape(1, 64),
        norm_gain.reshape(1, 64),
    )
    base, slope = station_terms(level_index, noisy, fresh_noise.reshape(8, 16, 256), got)
    result = outer(edges, *held, base, slope)
    return result.reshape(noisy_state.shape)


def solution(mesh):
    rest = (P(),) * 7
    placed = (
        P("tm", None, "space", None),
        P("tm", None, "space", None),
        P(),
        P("tm", None, "space"),
        P("space"),
        P("space", None),
        P("space"),
    ) + rest
    return jax.shard_map(
        local, mesh=mesh, in_specs=placed, out_specs=P("tm", None, "space", None), check_vma=False
    )
```

```python
import math

import jax
import jax.numpy as jnp
from jax import lax
from jax.experimental import pallas as pl
from jax.experimental.pallas import tpu as pltpu
from jax.sharding import PartitionSpec as P

LEVELS = 32
LEADER = 8
BF = jnp.bfloat16
F32 = jnp.float32
OUT_GROUP = 4
STATION_COST = 400_000_000
INNER_COST = 8_000_000_000
VM = pl.BlockSpec(memory_space=pltpu.VMEM)
SM = pl.BlockSpec(memory_space=pltpu.SMEM)


def scale_at(level, shape):
    steps = jnp.full(shape, level, jnp.int32).astype(F32)
    return 0.3 * jnp.exp(math.log(5.0) * steps / (LEVELS - 1))


def rolled(x, k):
    return pltpu.roll(x, k % x.shape[1], 1)


def parts_of(v):
    high = v.astype(BF)
    rest = v - high.astype(F32)
    middle = rest.astype(BF)
    low = (rest - middle.astype(F32)).astype(BF)
    return high, middle, low


def silu_half(h):
    return h + h * jnp.tanh(h)


def column_of(row):
    size = row.shape[1]
    line = lax.broadcasted_iota(jnp.int32, (size, size), 0)
    lane = lax.broadcasted_iota(jnp.int32, (size, size), 1)
    return jnp.sum(jnp.where(line == lane, row, 0.0), axis=1, keepdims=True)


def pack_body(level, noisy, obs, var, owner, cell, own, out, turned):
    count = obs.shape[2]
    peers = out.shape[0]
    noise = scale_at(level[0], (16, 256))
    inverse = 1.0 / jnp.sqrt(1.0 + noise * noise)
    for v in range(8):
        turned[:, v, :] = noisy[v] * inverse
    own[...] = turned[...].astype(BF)

    strip = owner[...]
    own_row = strip.astype(F32)
    own_col = column_of(own_row)
    row = lax.broadcasted_iota(jnp.int32, (count, count), 0)
    col = lax.broadcasted_iota(jnp.int32, (count, count), 1)
    same = (own_col == own_row) & (row < col)
    rank = jnp.sum(jnp.where(same, 1.0, 0.0), axis=0, keepdims=True)
    near = noise[:1, :count]
    weight = 1.0 / (var[...] + near * near)
    values = jnp.concatenate([obs[k] for k in range(obs.shape[0])], axis=0) * weight
    spot = cell[...]
    extra = [weight, (spot // 256).astype(F32), (spot % 256).astype(F32)]
    spare = jnp.zeros((16 - values.shape[0] - len(extra), count), F32)
    table = jnp.concatenate([values] + extra + [spare], axis=0)
    ranked = jnp.concatenate([jnp.where(rank == float(k), table, 0.0) for k in range(8)], axis=0)
    hot = jnp.where(
        lax.broadcasted_iota(jnp.int32, (peers, count), 0) == (strip + (peers - LEADER)) % peers, 1.0, 0.0
    ).astype(BF)
    total = None
    for part in parts_of(ranked):
        piece = lax.dot_general(
            hot, part, (((1,), (1,)), ((), ())), preferred_element_type=F32
        )
        total = piece if total is None else total + piece
    out[:, 0, :] = total


def pack(level, noisy, obs, var, owner, cell):
    return pl.pallas_call(
        pack_body,
        out_shape=(
            jax.ShapeDtypeStruct((16, 8, 256), BF),
            jax.ShapeDtypeStruct((64, 1, 128), F32),
        ),
        in_specs=[SM, VM, VM, VM, VM, VM],
        out_specs=(VM, VM),
        scratch_shapes=[pltpu.VMEM((16, 8, 256), F32)],
        cost_estimate=pl.CostEstimate(flops=50_000_000, bytes_accessed=400_000, transcendentals=0),
    )(level, noisy, obs, var, owner, cell)


def shifts(v):
    b = v.astype(BF)
    left, right = b[:, :256], b[:, 256:]
    return (
        jnp.concatenate([rolled(left, 1), rolled(right, 1)], 1),
        b,
        jnp.concatenate([rolled(left, -1), rolled(right, -1)], 1),
    )


def store_taps(x, row, taps):
    for k in range(3):
        at = row * 192 + k * 64
        x[at : at + 64, :] = taps[k]


def row_in(x1, row, even_t, o, a, b):
    o, a, b = o.astype(F32), a.astype(F32), b.astype(F32)
    before = jnp.where(even_t, b, a)
    later = jnp.where(even_t, a, b)
    tap_b, tap_o, tap_l = [(rolled(z, 1), z, rolled(z, -1)) for z in (before, o, later)]
    left = jnp.concatenate([z for k in range(3) for z in (tap_b[k], tap_o[k])], 0)
    right = jnp.concatenate([z for k in range(3) for z in (tap_o[k], tap_l[k])], 0)
    x1[row * 48 : (row + 1) * 48, :256] = left.astype(BF)
    x1[row * 48 : (row + 1) * 48, 256:] = right.astype(BF)


def first_rows(w1, bias, x1, x2, at, new):
    acc = jnp.dot(w1, x1[at * 48 : at * 48 + 240, :], preferred_element_type=F32)
    for r in range(3 - new, 3):
        store_taps(x2, at + r, shifts(silu_half(acc[r * 64 : (r + 1) * 64] + bias)))


def pieces_of(*sources):
    return [ref.at[(at + k) * 192 : (at + k + 1) * 192] for ref, at, rows in sources for k in range(rows)]


def summed(weight, pieces, done):
    held = []
    for y, piece in enumerate(pieces):
        held.append(jnp.dot(weight, piece[...], preferred_element_type=F32))
        if y >= 2:
            a, b, c = held[y - 2 :]
            done(y - 2, a[128:] + b[64:128] + c[:64])


def normed(m, gain):
    mean = jnp.sum(m * m, axis=0, keepdims=True) * (1 / 64)
    return silu_half(m * lax.rsqrt(mean + 1e-05) * gain)


def store_third(x4, row, f, h):
    third = (f.astype(F32) + silu_half(h)).astype(BF)
    x4[row * 128 : row * 128 + 64, :] = third[:, :256]
    x4[row * 128 + 64 : row * 128 + 128, :] = third[:, 256:]


def out_rows(wo, x4, at, den, row):
    size = OUT_GROUP * 8
    acc = jnp.dot(wo, x4[at * 128 : (at + OUT_GROUP + 2) * 128, :], preferred_element_type=F32)
    res = rolled(acc[:size], 1) + acc[size : 2 * size] + rolled(acc[2 * size :], -1)
    for r in range(OUT_GROUP):
        den[:, row + r, :] = res[r * 8 : (r + 1) * 8]


def station_body(level, noisy, fresh, got, base, slope):
    wide = got[:, 0, :].T
    table = jnp.concatenate([wide[k * 16 : (k + 1) * 16] for k in range(8)], axis=1)
    slots = table.shape[1]
    masks = (
        lax.broadcasted_iota(jnp.int32, (16, slots), 0) == table[9:10].astype(jnp.int32)
    )
    cols = jnp.where(
        lax.broadcasted_iota(jnp.int32, (256, slots), 0) == table[10:11].astype(jnp.int32),
        1.0,
        0.0,
    ).astype(BF)
    left = jnp.concatenate(
        [jnp.where(masks, table[v : v + 1], 0.0) for v in range(9)], axis=0
    )
    total = None
    for part in parts_of(left):
        piece = lax.dot_general(
            part, cols, (((1,), (1,)), ((), ())), preferred_element_type=F32
        )
        total = piece if total is None else total + piece
    scale = scale_at(level[0], (16, 256))
    after = scale_at(level[0] - 1, (16, 256))
    square = scale * scale
    weight = 1.0 - square * total[128:144]
    slope[...] = scale * weight
    for v in range(8):
        base[v] = noisy[v] * weight + square * total[v * 16 : (v + 1) * 16] + after * fresh[v]


def station_terms(level, noisy, fresh, got):
    return pl.pallas_call(
        station_body,
        out_shape=(
            jax.ShapeDtypeStruct((8, 16, 256), F32),
            jax.ShapeDtypeStruct((16, 256), F32),
        ),
        in_specs=[SM, VM, VM, VM],
        out_specs=(VM, VM),
        compiler_params=pltpu.CompilerParams(vmem_limit_bytes=16 * 2**20),
        cost_estimate=pl.CostEstimate(
            flops=STATION_COST, bytes_accessed=400_000, transcendentals=0
        ),
    )(level, noisy, fresh, got)


def inner_body(
    level,
    own,
    low,
    t2,
    high,
    conv_in,
    conv_mid,
    conv_res,
    conv_out,
    in_bias,
    noise_embed,
    norm_gain,
    w1_out,
    wm_out,
    wr_out,
    wo_out,
    columns,
    x1_edge,
    x2_edge,
    x3_edge,
    x4_edge,
    den,
    x1,
    x2,
    x3,
    x4,
):
    time_rank = lax.axis_index("tm")
    times = lax.axis_size("tm")
    even_t = time_rank % 2 == 0
    lower = time_rank < times // 2

    noise64 = scale_at(level[0], (1, 64))
    bias_row = 0.5 * (in_bias[...] + noise_embed[...] * jnp.log(10.0 * noise64))
    bias = column_of(bias_row)
    gain = column_of(0.5 * norm_gain[...])
    columns[0] = jnp.broadcast_to(bias, (64, 128))
    columns[1] = jnp.broadcast_to(gain, (64, 128))

    taps_in = [0.5 * conv_in[a].astype(F32).T for a in range(3)]
    spare = jnp.zeros((64, 48), F32)
    w1 = jnp.concatenate(
        [
            jnp.concatenate([taps_in[j - r] if 0 <= j - r < 3 else spare for j in range(5)], 1)
            for r in range(3)
        ],
        0,
    ).astype(BF)
    wm = jnp.concatenate([conv_mid[2], conv_mid[1], conv_mid[0]], 0)
    wr = (
        0.5 * jnp.concatenate([conv_res[2], conv_res[1], conv_res[0]], 0).astype(F32)
    ).astype(BF)
    coef0 = jnp.where(time_rank == 0, 0.0, jnp.where(time_rank == times - 1, 1.0, 0.5))
    coef1 = jnp.where(time_rank == 0, 1.0, jnp.where(time_rank == times - 1, 0.0, 0.5))
    tap_out = [conv_out[a].astype(F32) for a in range(3)]
    blank = jnp.zeros((8, 128), F32)
    banded = []
    for b in range(3):
        cell = [
            jnp.concatenate(
                [
                    coef0 * tap_out[a][8:, b * 64 : (b + 1) * 64],
                    coef1 * tap_out[a][:8, b * 64 : (b + 1) * 64],
                ],
                1,
            )
            for a in range(3)
        ]
        for r in range(OUT_GROUP):
            banded.append(
                jnp.concatenate(
                    [
                        cell[j - r] if 0 <= j - r < 3 else blank
                        for j in range(OUT_GROUP + 2)
                    ],
                    1,
                )
            )
    wo = jnp.concatenate(banded, 0).astype(BF)
    w1_out[...] = w1
    wm_out[...] = wm
    wr_out[...] = wr
    wo_out[...] = wo

    for y in range(16):
        row_in(x1, y, even_t, own[y], jnp.where(lower, low[y], high[y]), t2[y])
    for at, new in ((0, 3), (3, 3), (6, 3), (9, 3), (11, 2)):
        first_rows(w1, bias, x1, x2, at, new)
    summed(wm, pieces_of((x2, 0, 14)), lambda y, m: store_taps(x3, y, shifts(normed(m, gain))))

    def last(y, h):
        store_third(x4, y, x2[(y + 2) * 192 + 64 : (y + 2) * 192 + 128, :], h)

    summed(wr, pieces_of((x3, 0, 12)), last)
    for g in range(2):
        out_rows(wo, x4, g * 4, den, g * 4)
    x1_edge[:96] = x1[:96]
    x1_edge[96:] = x1[14 * 48 :]
    x2_edge[:384] = x2[:384]
    x2_edge[384:] = x2[12 * 192 :]
    x3_edge[:384] = x3[:384]
    x3_edge[384:] = x3[10 * 192 :]
    x4_edge[:256] = x4[:256]
    x4_edge[256:] = x4[8 * 128 :]


def inner(level, *arrays):
    return pl.pallas_call(
        inner_body,
        out_shape=(
            jax.ShapeDtypeStruct((192, 240), BF),
            jax.ShapeDtypeStruct((192, 192), BF),
            jax.ShapeDtypeStruct((192, 192), BF),
            jax.ShapeDtypeStruct((96, 768), BF),
            jax.ShapeDtypeStruct((2, 64, 128), F32),
            jax.ShapeDtypeStruct((4 * 48, 512), BF),
            jax.ShapeDtypeStruct((4 * 192, 512), BF),
            jax.ShapeDtypeStruct((4 * 192, 512), BF),
            jax.ShapeDtypeStruct((512, 256), BF),
            jax.ShapeDtypeStruct((8, 8, 256), F32),
        ),
        in_specs=[SM] + [VM] * 11,
        out_specs=(VM,) * 10,
        scratch_shapes=[
            pltpu.VMEM((16 * 48, 512), BF),
            pltpu.VMEM((14 * 192, 512), BF),
            pltpu.VMEM((12 * 192, 512), BF),
            pltpu.VMEM((10 * 128, 256), BF),
        ],
        compiler_params=pltpu.CompilerParams(vmem_limit_bytes=40 * 2**20),
        cost_estimate=pl.CostEstimate(
            flops=INNER_COST, bytes_accessed=1_000_000, transcendentals=2_000_000
        ),
    )(level, *arrays)


def outer_body(
    edges,
    w1,
    wm,
    wr,
    wo,
    columns,
    x1_edge,
    x2_edge,
    x3_edge,
    x4_edge,
    den_inner,
    base,
    slope,
    out,
    x1,
    x2,
    x3,
    x4,
    den,
):
    time_rank = lax.axis_index("tm")
    even_t = time_rank % 2 == 0
    lower = time_rank < lax.axis_size("tm") // 2
    even_s = lax.axis_index("space") % 2 == 0
    bias = columns[0][:, :1]
    gain = columns[1][:, :1]

    for y in range(4):
        u, v = edges[4 + y].astype(F32), edges[y].astype(F32)
        top = jnp.where(even_s, v, u)
        low = jnp.where(even_s, u, v)
        row_in(x1, y, even_t, top[:8], jnp.where(lower, top[8:16], top[24:]), top[16:24])
        row_in(x1, 8 + y, even_t, low[:8], jnp.where(lower, low[8:16], low[24:]), low[16:24])
    x1[4 * 48 : 8 * 48, :] = x1_edge[...]
    x4[4 * 128 : 8 * 128, :] = x4_edge[...]

    acc = [
        jnp.dot(w1[...], x1[at * 48 : at * 48 + 240, :], preferred_element_type=F32)
        for at in (0, 1, 6, 7)
    ]
    for row, k, r in (
        (0, 0, 0),
        (1, 0, 1),
        (2, 0, 2),
        (3, 1, 2),
        (4, 2, 0),
        (5, 2, 1),
        (6, 2, 2),
        (7, 3, 2),
    ):
        store_taps(x2, row, shifts(silu_half(acc[k][r * 64 : (r + 1) * 64] + bias)))

    def middle(at):
        return lambda y, m: store_taps(x3, at + y, shifts(normed(m, gain)))

    def last(at, ref, from_first, more):
        def done(y, h):
            source, row = (ref, from_first + y) if y < 2 else (more, y - 2)
            store_third(x4, at + y, source[row * 192 + 64 : row * 192 + 128, :], h)

        return done

    summed(wm[...], pieces_of((x2, 0, 4), (x2_edge, 0, 2)), middle(0))
    summed(wm[...], pieces_of((x2_edge, 2, 2), (x2, 4, 4)), middle(4))
    summed(wr[...], pieces_of((x3, 0, 4), (x3_edge, 0, 2)), last(0, x2, 2, x2_edge))
    summed(wr[...], pieces_of((x3_edge, 2, 2), (x3, 4, 4)), last(8, x2_edge, 2, x2.at[4 * 192 :]))
    out_rows(wo[...], x4, 0, den, 0)
    den[:, 4:12, :] = den_inner[...]
    out_rows(wo[...], x4, 6, den, 12)

    for v in range(8):
        out[v] = base[v] - slope[...] * den[v]


def outer(*arrays):
    return pl.pallas_call(
        outer_body,
        out_shape=jax.ShapeDtypeStruct((8, 16, 256), F32),
        in_specs=[VM] * 13,
        out_specs=VM,
        scratch_shapes=[
            pltpu.VMEM((12 * 48, 512), BF),
            pltpu.VMEM((8 * 192, 512), BF),
            pltpu.VMEM((8 * 192, 512), BF),
            pltpu.VMEM((12 * 128, 256), BF),
            pltpu.VMEM((8, 16, 256), F32),
        ],
        compiler_params=pltpu.CompilerParams(vmem_limit_bytes=40 * 2**20),
        cost_estimate=pl.CostEstimate(
            flops=4_000_000_000, bytes_accessed=1_000_000, transcendentals=1_000_000
        ),
    )(*arrays)


def order_of(count):
    return [(k + LEADER) % count for k in range(count)]


def swapped(value, axis, first, stop=None):
    count = lax.axis_size(axis)
    wrap = axis == "space"
    pairs = []
    for i in range(first, count if wrap else stop or count - 1, 2):
        j = (i + 1) % count
        pairs += [(i, j), (j, i)]
    return lax.ppermute(value, axis, pairs)


def local(
    noisy_state,
    fresh_noise,
    level_index,
    station_obs,
    obs_variance,
    station_owner,
    station_cell,
    conv_in,
    conv_mid,
    conv_res,
    conv_out,
    in_bias,
    noise_embed,
    norm_gain,
):
    even_s = lax.axis_index("space") % 2 == 0
    noisy = noisy_state.reshape(8, 16, 256)
    own, slots = pack(
        level_index,
        noisy,
        station_obs,
        obs_variance.reshape(1, 128),
        station_owner.reshape(1, 128),
        station_cell.reshape(1, 128),
    )
    half = lax.axis_size("tm") // 2
    low = swapped(own, "tm", 0, half)
    t2 = swapped(own, "tm", 1)
    high = swapped(own, "tm", half)
    got = lax.all_to_all(
        slots, "space", 0, 0, axis_index_groups=[order_of(slots.shape[0])], tiled=True
    )

    edge = jnp.where(even_s, 12, 0)
    both = jnp.concatenate([own, low, t2, high], axis=1)
    m2 = swapped(lax.dynamic_slice_in_dim(both, 12 - edge, 4, 0), "space", 1)
    m1 = swapped(lax.dynamic_slice_in_dim(both, edge, 4, 0), "space", 0)

    edges = jnp.concatenate([m2, m1], axis=0)
    held = inner(
        level_index,
        own,
        low,
        t2,
        high,
        conv_in.transpose(0, 2, 1),
        conv_mid,
        conv_res,
        conv_out,
        in_bias.reshape(1, 64),
        noise_embed.reshape(1, 64),
        norm_gain.reshape(1, 64),
    )
    base, slope = station_terms(level_index, noisy, fresh_noise.reshape(8, 16, 256), got)
    result = outer(edges, *held, base, slope)
    return result.reshape(noisy_state.shape)


def solution(mesh):
    rest = (P(),) * 7
    placed = (
        P("tm", None, "space", None),
        P("tm", None, "space", None),
        P(),
        P("tm", None, "space"),
        P("space"),
        P("space", None),
        P("space"),
    ) + rest
    return jax.shard_map(
        local, mesh=mesh, in_specs=placed, out_specs=P("tm", None, "space", None), check_vma=False
    )
```

```python
import math

import jax
import jax.numpy as jnp
from jax import lax
from jax.experimental import pallas as pl
from jax.experimental.pallas import tpu as pltpu
from jax.sharding import PartitionSpec as P

LEVELS = 32
LEADER = 6
BF = jnp.bfloat16
F32 = jnp.float32
OUT_GROUP = 4
STATION_COST = 400_000_000
INNER_COST = 8_000_000_000
VM = pl.BlockSpec(memory_space=pltpu.VMEM)
SM = pl.BlockSpec(memory_space=pltpu.SMEM)


def scale_at(level, shape):
    steps = jnp.full(shape, level, jnp.int32).astype(F32)
    return 0.3 * jnp.exp(math.log(5.0) * steps / (LEVELS - 1))


def rolled(x, k):
    return pltpu.roll(x, k % x.shape[1], 1)


def parts_of(v):
    high = v.astype(BF)
    rest = v - high.astype(F32)
    middle = rest.astype(BF)
    low = (rest - middle.astype(F32)).astype(BF)
    return high, middle, low


def silu_half(h):
    return h + h * jnp.tanh(h)


def column_of(row):
    size = row.shape[1]
    line = lax.broadcasted_iota(jnp.int32, (size, size), 0)
    lane = lax.broadcasted_iota(jnp.int32, (size, size), 1)
    return jnp.sum(jnp.where(line == lane, row, 0.0), axis=1, keepdims=True)


def pack_body(
    level, noisy, obs, var, owner, cell, in_bias, noise_embed, norm_gain, own, out, columns, turned
):
    count = obs.shape[2]
    peers = out.shape[0]
    noise = scale_at(level[0], (16, 256))
    inverse = 1.0 / jnp.sqrt(1.0 + noise * noise)
    for v in range(8):
        turned[:, v, :] = noisy[v] * inverse
    own[...] = turned[...].astype(BF)

    strip = owner[...]
    own_row = strip.astype(F32)
    own_col = column_of(own_row)
    row = lax.broadcasted_iota(jnp.int32, (count, count), 0)
    col = lax.broadcasted_iota(jnp.int32, (count, count), 1)
    same = (own_col == own_row) & (row < col)
    rank = jnp.sum(jnp.where(same, 1.0, 0.0), axis=0, keepdims=True)
    near = noise[:1, :count]
    weight = 1.0 / (var[...] + near * near)
    values = jnp.concatenate([obs[k] for k in range(obs.shape[0])], axis=0) * weight
    spot = cell[...]
    extra = [weight, (spot // 256).astype(F32), (spot % 256).astype(F32)]
    spare = jnp.zeros((16 - values.shape[0] - len(extra), count), F32)
    table = jnp.concatenate([values] + extra + [spare], axis=0)
    ranked = jnp.concatenate([jnp.where(rank == float(k), table, 0.0) for k in range(8)], axis=0)
    hot = jnp.where(
        lax.broadcasted_iota(jnp.int32, (peers, count), 0) == (strip + (peers - LEADER)) % peers, 1.0, 0.0
    ).astype(BF)
    total = None
    for part in parts_of(ranked):
        piece = lax.dot_general(
            hot, part, (((1,), (1,)), ((), ())), preferred_element_type=F32
        )
        total = piece if total is None else total + piece
    out[:, 0, :] = total

    bias = 0.5 * (in_bias[...] + noise_embed[...] * jnp.log(10.0 * noise[:1, :64]))
    columns[0] = jnp.broadcast_to(column_of(bias), (64, 128))
    columns[1] = jnp.broadcast_to(column_of(0.5 * norm_gain[...]), (64, 128))


def pack(level, *arrays):
    return pl.pallas_call(
        pack_body,
        out_shape=(
            jax.ShapeDtypeStruct((16, 8, 256), BF),
            jax.ShapeDtypeStruct((64, 1, 128), F32),
            jax.ShapeDtypeStruct((2, 64, 128), F32),
        ),
        in_specs=[SM] + [VM] * 8,
        out_specs=(VM, VM, VM),
        scratch_shapes=[pltpu.VMEM((16, 8, 256), F32)],
        cost_estimate=pl.CostEstimate(flops=50_000_000, bytes_accessed=400_000, transcendentals=0),
    )(level, *arrays)


def shifts(v):
    b = v.astype(BF)
    left, right = b[:, :256], b[:, 256:]
    return (
        jnp.concatenate([rolled(left, 1), rolled(right, 1)], 1),
        b,
        jnp.concatenate([rolled(left, -1), rolled(right, -1)], 1),
    )


def store_taps(x, row, taps):
    for k in range(3):
        at = row * 192 + k * 64
        x[at : at + 64, :] = taps[k]


def row_in(x1, row, even_t, o, a, b):
    o, a, b = o.astype(F32), a.astype(F32), b.astype(F32)
    before = jnp.where(even_t, b, a)
    later = jnp.where(even_t, a, b)
    tap_b, tap_o, tap_l = [(rolled(z, 1), z, rolled(z, -1)) for z in (before, o, later)]
    left = jnp.concatenate([z for k in range(3) for z in (tap_b[k], tap_o[k])], 0)
    right = jnp.concatenate([z for k in range(3) for z in (tap_o[k], tap_l[k])], 0)
    x1[row * 48 : (row + 1) * 48, :256] = left.astype(BF)
    x1[row * 48 : (row + 1) * 48, 256:] = right.astype(BF)


def first_rows(w1, bias, x1, x2, at, new):
    acc = jnp.dot(w1, x1[at * 48 : at * 48 + 240, :], preferred_element_type=F32)
    for r in range(3 - new, 3):
        store_taps(x2, at + r, shifts(silu_half(acc[r * 64 : (r + 1) * 64] + bias)))


def pieces_of(*sources):
    return [ref.at[(at + k) * 192 : (at + k + 1) * 192] for ref, at, rows in sources for k in range(rows)]


def summed(weight, pieces, done):
    held = []
    for y, piece in enumerate(pieces):
        held.append(jnp.dot(weight, piece[...], preferred_element_type=F32))
        if y >= 2:
            a, b, c = held[y - 2 :]
            done(y - 2, a[128:] + b[64:128] + c[:64])


def normed(m, gain):
    mean = jnp.sum(m * m, axis=0, keepdims=True) * (1 / 64)
    return silu_half(m * lax.rsqrt(mean + 1e-05) * gain)


def store_third(x4, row, f, h):
    third = (f.astype(F32) + silu_half(h)).astype(BF)
    x4[row * 128 : row * 128 + 64, :] = third[:, :256]
    x4[row * 128 + 64 : row * 128 + 128, :] = third[:, 256:]


def out_rows(wo, x4, at, den, row):
    size = OUT_GROUP * 8
    acc = jnp.dot(wo, x4[at * 128 : (at + OUT_GROUP + 2) * 128, :], preferred_element_type=F32)
    res = rolled(acc[:size], 1) + acc[size : 2 * size] + rolled(acc[2 * size :], -1)
    for r in range(OUT_GROUP):
        den[:, row + r, :] = res[r * 8 : (r + 1) * 8]


def station_body(level, noisy, fresh, got, base, slope):
    wide = got[:, 0, :].T
    table = jnp.concatenate([wide[k * 16 : (k + 1) * 16] for k in range(8)], axis=1)
    slots = table.shape[1]
    masks = (
        lax.broadcasted_iota(jnp.int32, (16, slots), 0) == table[9:10].astype(jnp.int32)
    )
    cols = jnp.where(
        lax.broadcasted_iota(jnp.int32, (256, slots), 0) == table[10:11].astype(jnp.int32),
        1.0,
        0.0,
    ).astype(BF)
    left = jnp.concatenate(
        [jnp.where(masks, table[v : v + 1], 0.0) for v in range(9)], axis=0
    )
    total = None
    for part in parts_of(left):
        piece = lax.dot_general(
            part, cols, (((1,), (1,)), ((), ())), preferred_element_type=F32
        )
        total = piece if total is None else total + piece
    scale = scale_at(level[0], (16, 256))
    after = scale_at(level[0] - 1, (16, 256))
    square = scale * scale
    weight = 1.0 - square * total[128:144]
    slope[...] = scale * weight
    for v in range(8):
        base[v] = noisy[v] * weight + square * total[v * 16 : (v + 1) * 16] + after * fresh[v]


def station_terms(level, noisy, fresh, got):
    return pl.pallas_call(
        station_body,
        out_shape=(
            jax.ShapeDtypeStruct((8, 16, 256), F32),
            jax.ShapeDtypeStruct((16, 256), F32),
        ),
        in_specs=[SM, VM, VM, VM],
        out_specs=(VM, VM),
        compiler_params=pltpu.CompilerParams(vmem_limit_bytes=16 * 2**20),
        cost_estimate=pl.CostEstimate(
            flops=STATION_COST, bytes_accessed=400_000, transcendentals=0
        ),
    )(level, noisy, fresh, got)


def inner_body(
    level,
    own,
    low,
    t2,
    high,
    conv_in,
    conv_mid,
    conv_res,
    conv_out,
    columns,
    w1_out,
    wm_out,
    wr_out,
    wo_out,
    x1_edge,
    x2_edge,
    x3_edge,
    x4_edge,
    den,
    x1,
    x2,
    x3,
    x4,
):
    time_rank = lax.axis_index("tm")
    times = lax.axis_size("tm")
    even_t = time_rank % 2 == 0
    lower = time_rank < times // 2

    bias = columns[0][:, :1]
    gain = columns[1][:, :1]

    taps_in = [0.5 * conv_in[a].astype(F32).T for a in range(3)]
    spare = jnp.zeros((64, 48), F32)
    w1 = jnp.concatenate(
        [
            jnp.concatenate([taps_in[j - r] if 0 <= j - r < 3 else spare for j in range(5)], 1)
            for r in range(3)
        ],
        0,
    ).astype(BF)
    wm = jnp.concatenate([conv_mid[2], conv_mid[1], conv_mid[0]], 0)
    wr = (
        0.5 * jnp.concatenate([conv_res[2], conv_res[1], conv_res[0]], 0).astype(F32)
    ).astype(BF)
    coef0 = jnp.where(time_rank == 0, 0.0, jnp.where(time_rank == times - 1, 1.0, 0.5))
    coef1 = jnp.where(time_rank == 0, 1.0, jnp.where(time_rank == times - 1, 0.0, 0.5))
    tap_out = [conv_out[a].astype(F32) for a in range(3)]
    blank = jnp.zeros((8, 128), F32)
    banded = []
    for b in range(3):
        cell = [
            jnp.concatenate(
                [
                    coef0 * tap_out[a][8:, b * 64 : (b + 1) * 64],
                    coef1 * tap_out[a][:8, b * 64 : (b + 1) * 64],
                ],
                1,
            )
            for a in range(3)
        ]
        for r in range(OUT_GROUP):
            banded.append(
                jnp.concatenate(
                    [
                        cell[j - r] if 0 <= j - r < 3 else blank
                        for j in range(OUT_GROUP + 2)
                    ],
                    1,
                )
            )
    wo = jnp.concatenate(banded, 0).astype(BF)
    w1_out[...] = w1
    wm_out[...] = wm
    wr_out[...] = wr
    wo_out[...] = wo

    for y in range(16):
        row_in(x1, y, even_t, own[y], jnp.where(lower, low[y], high[y]), t2[y])
    for at, new in ((0, 3), (3, 3), (6, 3), (9, 3), (11, 2)):
        first_rows(w1, bias, x1, x2, at, new)
    summed(wm, pieces_of((x2, 0, 14)), lambda y, m: store_taps(x3, y, shifts(normed(m, gain))))

    def last(y, h):
        store_third(x4, y, x2[(y + 2) * 192 + 64 : (y + 2) * 192 + 128, :], h)

    summed(wr, pieces_of((x3, 0, 12)), last)
    for g in range(2):
        out_rows(wo, x4, g * 4, den, g * 4)
    x1_edge[:96] = x1[:96]
    x1_edge[96:] = x1[14 * 48 :]
    x2_edge[:384] = x2[:384]
    x2_edge[384:] = x2[12 * 192 :]
    x3_edge[:384] = x3[:384]
    x3_edge[384:] = x3[10 * 192 :]
    x4_edge[:256] = x4[:256]
    x4_edge[256:] = x4[8 * 128 :]


def inner(level, *arrays):
    return pl.pallas_call(
        inner_body,
        out_shape=(
            jax.ShapeDtypeStruct((192, 240), BF),
            jax.ShapeDtypeStruct((192, 192), BF),
            jax.ShapeDtypeStruct((192, 192), BF),
            jax.ShapeDtypeStruct((96, 768), BF),
            jax.ShapeDtypeStruct((4 * 48, 512), BF),
            jax.ShapeDtypeStruct((4 * 192, 512), BF),
            jax.ShapeDtypeStruct((4 * 192, 512), BF),
            jax.ShapeDtypeStruct((512, 256), BF),
            jax.ShapeDtypeStruct((8, 8, 256), F32),
        ),
        in_specs=[SM] + [VM] * 9,
        out_specs=(VM,) * 9,
        scratch_shapes=[
            pltpu.VMEM((16 * 48, 512), BF),
            pltpu.VMEM((14 * 192, 512), BF),
            pltpu.VMEM((12 * 192, 512), BF),
            pltpu.VMEM((10 * 128, 256), BF),
        ],
        compiler_params=pltpu.CompilerParams(vmem_limit_bytes=40 * 2**20),
        cost_estimate=pl.CostEstimate(
            flops=INNER_COST, bytes_accessed=1_000_000, transcendentals=2_000_000
        ),
    )(level, *arrays)


def outer_body(
    edges,
    w1,
    wm,
    wr,
    wo,
    columns,
    x1_edge,
    x2_edge,
    x3_edge,
    x4_edge,
    den_inner,
    base,
    slope,
    out,
    x1,
    x2,
    x3,
    x4,
    den,
):
    time_rank = lax.axis_index("tm")
    even_t = time_rank % 2 == 0
    lower = time_rank < lax.axis_size("tm") // 2
    even_s = lax.axis_index("space") % 2 == 0
    bias = columns[0][:, :1]
    gain = columns[1][:, :1]

    for y in range(4):
        u, v = edges[4 + y].astype(F32), edges[y].astype(F32)
        top = jnp.where(even_s, v, u)
        low = jnp.where(even_s, u, v)
        row_in(x1, y, even_t, top[:8], jnp.where(lower, top[8:16], top[24:]), top[16:24])
        row_in(x1, 8 + y, even_t, low[:8], jnp.where(lower, low[8:16], low[24:]), low[16:24])
    x1[4 * 48 : 8 * 48, :] = x1_edge[...]
    x4[4 * 128 : 8 * 128, :] = x4_edge[...]

    acc = [
        jnp.dot(w1[...], x1[at * 48 : at * 48 + 240, :], preferred_element_type=F32)
        for at in (0, 1, 6, 7)
    ]
    for row, k, r in (
        (0, 0, 0),
        (1, 0, 1),
        (2, 0, 2),
        (3, 1, 2),
        (4, 2, 0),
        (5, 2, 1),
        (6, 2, 2),
        (7, 3, 2),
    ):
        store_taps(x2, row, shifts(silu_half(acc[k][r * 64 : (r + 1) * 64] + bias)))

    def middle(at):
        return lambda y, m: store_taps(x3, at + y, shifts(normed(m, gain)))

    def last(at, ref, from_first, more):
        def done(y, h):
            source, row = (ref, from_first + y) if y < 2 else (more, y - 2)
            store_third(x4, at + y, source[row * 192 + 64 : row * 192 + 128, :], h)

        return done

    summed(wm[...], pieces_of((x2, 0, 4), (x2_edge, 0, 2)), middle(0))
    summed(wm[...], pieces_of((x2_edge, 2, 2), (x2, 4, 4)), middle(4))
    summed(wr[...], pieces_of((x3, 0, 4), (x3_edge, 0, 2)), last(0, x2, 2, x2_edge))
    summed(wr[...], pieces_of((x3_edge, 2, 2), (x3, 4, 4)), last(8, x2_edge, 2, x2.at[4 * 192 :]))
    out_rows(wo[...], x4, 0, den, 0)
    den[:, 4:12, :] = den_inner[...]
    out_rows(wo[...], x4, 6, den, 12)

    for v in range(8):
        out[v] = base[v] - slope[...] * den[v]


def outer(*arrays):
    return pl.pallas_call(
        outer_body,
        out_shape=jax.ShapeDtypeStruct((8, 16, 256), F32),
        in_specs=[VM] * 13,
        out_specs=VM,
        scratch_shapes=[
            pltpu.VMEM((12 * 48, 512), BF),
            pltpu.VMEM((8 * 192, 512), BF),
            pltpu.VMEM((8 * 192, 512), BF),
            pltpu.VMEM((12 * 128, 256), BF),
            pltpu.VMEM((8, 16, 256), F32),
        ],
        compiler_params=pltpu.CompilerParams(vmem_limit_bytes=40 * 2**20),
        cost_estimate=pl.CostEstimate(
            flops=4_000_000_000, bytes_accessed=1_000_000, transcendentals=1_000_000
        ),
    )(*arrays)


def order_of(count):
    return [(k + LEADER) % count for k in range(count)]


def swapped(value, axis, first, stop=None):
    count = lax.axis_size(axis)
    wrap = axis == "space"
    pairs = []
    for i in range(first, count if wrap else stop or count - 1, 2):
        j = (i + 1) % count
        pairs += [(i, j), (j, i)]
    return lax.ppermute(value, axis, pairs)


def local(
    noisy_state,
    fresh_noise,
    level_index,
    station_obs,
    obs_variance,
    station_owner,
    station_cell,
    conv_in,
    conv_mid,
    conv_res,
    conv_out,
    in_bias,
    noise_embed,
    norm_gain,
):
    even_s = lax.axis_index("space") % 2 == 0
    noisy = noisy_state.reshape(8, 16, 256)
    own, slots, columns = pack(
        level_index,
        noisy,
        station_obs,
        obs_variance.reshape(1, 128),
        station_owner.reshape(1, 128),
        station_cell.reshape(1, 128),
        in_bias.reshape(1, 64),
        noise_embed.reshape(1, 64),
        norm_gain.reshape(1, 64),
    )
    half = lax.axis_size("tm") // 2
    low = swapped(own, "tm", 0, half)
    t2 = swapped(own, "tm", 1)
    high = swapped(own, "tm", half)
    got = lax.all_to_all(
        slots, "space", 0, 0, axis_index_groups=[order_of(slots.shape[0])], tiled=True
    )

    edge = jnp.where(even_s, 12, 0)
    both = jnp.concatenate([own, low, t2, high], axis=1)
    m2 = swapped(lax.dynamic_slice_in_dim(both, 12 - edge, 4, 0), "space", 1)
    m1 = swapped(lax.dynamic_slice_in_dim(both, edge, 4, 0), "space", 0)

    edges = jnp.concatenate([m2, m1], axis=0)
    held = inner(
        level_index,
        own,
        low,
        t2,
        high,
        conv_in.transpose(0, 2, 1),
        conv_mid,
        conv_res,
        conv_out,
        columns,
    )
    base, slope = station_terms(level_index, noisy, fresh_noise.reshape(8, 16, 256), got)
    result = outer(edges, *held[:4], columns, *held[4:], base, slope)
    return result.reshape(noisy_state.shape)


def solution(mesh):
    rest = (P(),) * 7
    placed = (
        P("tm", None, "space", None),
        P("tm", None, "space", None),
        P(),
        P("tm", None, "space"),
        P("space"),
        P("space", None),
        P("space"),
    ) + rest
    return jax.shard_map(
        local, mesh=mesh, in_specs=placed, out_specs=P("tm", None, "space", None), check_vma=False
    )
```

```python
import math

import jax
import jax.numpy as jnp
from jax import lax
from jax.experimental import pallas as pl
from jax.experimental.pallas import tpu as pltpu
from jax.sharding import PartitionSpec as P

LEVELS = 32
LEADER = 6
BF = jnp.bfloat16
F32 = jnp.float32
OUT_GROUP = 4
STATION_COST = 400_000_000
INNER_COST = 8_000_000_000
VM = pl.BlockSpec(memory_space=pltpu.VMEM)
SM = pl.BlockSpec(memory_space=pltpu.SMEM)


def scale_at(level, shape):
    steps = jnp.full(shape, level, jnp.int32).astype(F32)
    return 0.3 * jnp.exp(math.log(5.0) * steps / (LEVELS - 1))


def rolled(x, k):
    return pltpu.roll(x, k % x.shape[1], 1)


def parts_of(v):
    high = v.astype(BF)
    rest = v - high.astype(F32)
    middle = rest.astype(BF)
    low = (rest - middle.astype(F32)).astype(BF)
    return high, middle, low


def silu_half(h):
    return h + h * jnp.tanh(h)


def column_of(row):
    size = row.shape[1]
    line = lax.broadcasted_iota(jnp.int32, (size, size), 0)
    lane = lax.broadcasted_iota(jnp.int32, (size, size), 1)
    return jnp.sum(jnp.where(line == lane, row, 0.0), axis=1, keepdims=True)


def pack_body(
    level, noisy, obs, var, owner, cell, in_bias, noise_embed, norm_gain, own, out, columns, turned
):
    count = obs.shape[2]
    peers = out.shape[0]
    noise = scale_at(level[0], (16, 256))
    inverse = 1.0 / jnp.sqrt(1.0 + noise * noise)
    for v in range(8):
        turned[:, v, :] = noisy[v] * inverse
    own[...] = turned[...].astype(BF)

    strip = owner[...]
    own_row = strip.astype(F32)
    own_col = column_of(own_row)
    row = lax.broadcasted_iota(jnp.int32, (count, count), 0)
    col = lax.broadcasted_iota(jnp.int32, (count, count), 1)
    same = (own_col == own_row) & (row < col)
    rank = jnp.sum(jnp.where(same, 1.0, 0.0), axis=0, keepdims=True)
    near = noise[:1, :count]
    weight = 1.0 / (var[...] + near * near)
    values = jnp.concatenate([obs[k] for k in range(obs.shape[0])], axis=0) * weight
    spot = cell[...]
    extra = [weight, (spot // 256).astype(F32), (spot % 256).astype(F32)]
    spare = jnp.zeros((16 - values.shape[0] - len(extra), count), F32)
    table = jnp.concatenate([values] + extra + [spare], axis=0)
    ranked = jnp.concatenate([jnp.where(rank == float(k), table, 0.0) for k in range(8)], axis=0)
    hot = jnp.where(
        lax.broadcasted_iota(jnp.int32, (peers, count), 0) == (strip + (peers - LEADER)) % peers, 1.0, 0.0
    ).astype(BF)
    stacked = jnp.concatenate(parts_of(ranked), axis=0)
    pieces = lax.dot_general(
        hot, stacked, (((1,), (1,)), ((), ())), preferred_element_type=F32
    )
    total = pieces[:, :128] + pieces[:, 128:256] + pieces[:, 256:]
    out[:, 0, :] = total

    bias = 0.5 * (in_bias[...] + noise_embed[...] * jnp.log(10.0 * noise[:1, :64]))
    columns[0] = jnp.broadcast_to(column_of(bias), (64, 128))
    columns[1] = jnp.broadcast_to(column_of(0.5 * norm_gain[...]), (64, 128))


def pack(level, *arrays):
    return pl.pallas_call(
        pack_body,
        out_shape=(
            jax.ShapeDtypeStruct((16, 8, 256), BF),
            jax.ShapeDtypeStruct((64, 1, 128), F32),
            jax.ShapeDtypeStruct((2, 64, 128), F32),
        ),
        in_specs=[SM] + [VM] * 8,
        out_specs=(VM, VM, VM),
        scratch_shapes=[pltpu.VMEM((16, 8, 256), F32)],
        cost_estimate=pl.CostEstimate(flops=50_000_000, bytes_accessed=400_000, transcendentals=0),
    )(level, *arrays)


def shifts(v):
    b = v.astype(BF)
    left, right = b[:, :256], b[:, 256:]
    return (
        jnp.concatenate([rolled(left, 1), rolled(right, 1)], 1),
        b,
        jnp.concatenate([rolled(left, -1), rolled(right, -1)], 1),
    )


def store_taps(x, row, taps):
    for k in range(3):
        at = row * 192 + k * 64
        x[at : at + 64, :] = taps[k]


def row_in(x1, row, even_t, o, a, b):
    o, a, b = o.astype(F32), a.astype(F32), b.astype(F32)
    before = jnp.where(even_t, b, a)
    later = jnp.where(even_t, a, b)
    tap_b, tap_o, tap_l = [(rolled(z, 1), z, rolled(z, -1)) for z in (before, o, later)]
    left = jnp.concatenate([z for k in range(3) for z in (tap_b[k], tap_o[k])], 0)
    right = jnp.concatenate([z for k in range(3) for z in (tap_o[k], tap_l[k])], 0)
    x1[row * 48 : (row + 1) * 48, :256] = left.astype(BF)
    x1[row * 48 : (row + 1) * 48, 256:] = right.astype(BF)


def first_rows(w1, bias, x1, x2, at, new):
    acc = jnp.dot(w1, x1[at * 48 : at * 48 + 240, :], preferred_element_type=F32)
    for r in range(3 - new, 3):
        store_taps(x2, at + r, shifts(silu_half(acc[r * 64 : (r + 1) * 64] + bias)))


def pieces_of(*sources):
    return [ref.at[(at + k) * 192 : (at + k + 1) * 192] for ref, at, rows in sources for k in range(rows)]


def summed(weight, pieces, done):
    held = []
    for y, piece in enumerate(pieces):
        held.append(jnp.dot(weight, piece[...], preferred_element_type=F32))
        if y >= 2:
            a, b, c = held[y - 2 :]
            done(y - 2, a[128:] + b[64:128] + c[:64])


def normed(m, gain):
    mean = jnp.sum(m * m, axis=0, keepdims=True) * (1 / 64)
    return silu_half(m * lax.rsqrt(mean + 1e-05) * gain)


def store_third(x4, row, f, h):
    third = (f.astype(F32) + silu_half(h)).astype(BF)
    x4[row * 128 : row * 128 + 64, :] = third[:, :256]
    x4[row * 128 + 64 : row * 128 + 128, :] = third[:, 256:]


def out_rows(wo, x4, at, den, row):
    size = OUT_GROUP * 8
    acc = jnp.dot(wo, x4[at * 128 : (at + OUT_GROUP + 2) * 128, :], preferred_element_type=F32)
    res = rolled(acc[:size], 1) + acc[size : 2 * size] + rolled(acc[2 * size :], -1)
    for r in range(OUT_GROUP):
        den[:, row + r, :] = res[r * 8 : (r + 1) * 8]


def station_body(level, noisy, fresh, got, base, slope):
    wide = got[:, 0, :].T
    table = jnp.concatenate([wide[k * 16 : (k + 1) * 16] for k in range(8)], axis=1)
    slots = table.shape[1]
    masks = (
        lax.broadcasted_iota(jnp.int32, (16, slots), 0) == table[9:10].astype(jnp.int32)
    )
    cols = jnp.where(
        lax.broadcasted_iota(jnp.int32, (256, slots), 0) == table[10:11].astype(jnp.int32),
        1.0,
        0.0,
    ).astype(BF)
    left = jnp.concatenate(
        [jnp.where(masks, table[v : v + 1], 0.0) for v in range(9)], axis=0
    )
    stacked = jnp.concatenate(parts_of(left), axis=0)
    pieces = lax.dot_general(
        stacked, cols, (((1,), (1,)), ((), ())), preferred_element_type=F32
    )
    total = pieces[:144] + pieces[144:288] + pieces[288:]
    scale = scale_at(level[0], (16, 256))
    after = scale_at(level[0] - 1, (16, 256))
    square = scale * scale
    weight = 1.0 - square * total[128:144]
    slope[...] = scale * weight
    for v in range(8):
        base[v] = noisy[v] * weight + square * total[v * 16 : (v + 1) * 16] + after * fresh[v]


def station_terms(level, noisy, fresh, got):
    return pl.pallas_call(
        station_body,
        out_shape=(
            jax.ShapeDtypeStruct((8, 16, 256), F32),
            jax.ShapeDtypeStruct((16, 256), F32),
        ),
        in_specs=[SM, VM, VM, VM],
        out_specs=(VM, VM),
        compiler_params=pltpu.CompilerParams(vmem_limit_bytes=16 * 2**20),
        cost_estimate=pl.CostEstimate(
            flops=STATION_COST, bytes_accessed=400_000, transcendentals=0
        ),
    )(level, noisy, fresh, got)


def inner_body(
    level,
    own,
    low,
    t2,
    high,
    conv_in,
    conv_mid,
    conv_res,
    conv_out,
    columns,
    w1_out,
    wm_out,
    wr_out,
    wo_out,
    x1_edge,
    x2_edge,
    x3_edge,
    x4_edge,
    den,
    x1,
    x2,
    x3,
    x4,
):
    time_rank = lax.axis_index("tm")
    times = lax.axis_size("tm")
    even_t = time_rank % 2 == 0
    lower = time_rank < times // 2

    bias = columns[0][:, :1]
    gain = columns[1][:, :1]

    taps_in = [0.5 * conv_in[a].astype(F32).T for a in range(3)]
    spare = jnp.zeros((64, 48), F32)
    w1 = jnp.concatenate(
        [
            jnp.concatenate([taps_in[j - r] if 0 <= j - r < 3 else spare for j in range(5)], 1)
            for r in range(3)
        ],
        0,
    ).astype(BF)
    wm = jnp.concatenate([conv_mid[2], conv_mid[1], conv_mid[0]], 0)
    wr = (
        0.5 * jnp.concatenate([conv_res[2], conv_res[1], conv_res[0]], 0).astype(F32)
    ).astype(BF)
    coef0 = jnp.where(time_rank == 0, 0.0, jnp.where(time_rank == times - 1, 1.0, 0.5))
    coef1 = jnp.where(time_rank == 0, 1.0, jnp.where(time_rank == times - 1, 0.0, 0.5))
    tap_out = [conv_out[a].astype(F32) for a in range(3)]
    blank = jnp.zeros((8, 128), F32)
    banded = []
    for b in range(3):
        cell = [
            jnp.concatenate(
                [
                    coef0 * tap_out[a][8:, b * 64 : (b + 1) * 64],
                    coef1 * tap_out[a][:8, b * 64 : (b + 1) * 64],
                ],
                1,
            )
            for a in range(3)
        ]
        for r in range(OUT_GROUP):
            banded.append(
                jnp.concatenate(
                    [
                        cell[j - r] if 0 <= j - r < 3 else blank
                        for j in range(OUT_GROUP + 2)
                    ],
                    1,
                )
            )
    wo = jnp.concatenate(banded, 0).astype(BF)
    w1_out[...] = w1
    wm_out[...] = wm
    wr_out[...] = wr
    wo_out[...] = wo

    for y in range(16):
        row_in(x1, y, even_t, own[y], jnp.where(lower, low[y], high[y]), t2[y])
    for at, new in ((0, 3), (3, 3), (6, 3), (9, 3), (11, 2)):
        first_rows(w1, bias, x1, x2, at, new)
    summed(wm, pieces_of((x2, 0, 14)), lambda y, m: store_taps(x3, y, shifts(normed(m, gain))))

    def last(y, h):
        store_third(x4, y, x2[(y + 2) * 192 + 64 : (y + 2) * 192 + 128, :], h)

    summed(wr, pieces_of((x3, 0, 12)), last)
    for g in range(2):
        out_rows(wo, x4, g * 4, den, g * 4)
    x1_edge[:96] = x1[:96]
    x1_edge[96:] = x1[14 * 48 :]
    x2_edge[:384] = x2[:384]
    x2_edge[384:] = x2[12 * 192 :]
    x3_edge[:384] = x3[:384]
    x3_edge[384:] = x3[10 * 192 :]
    x4_edge[:256] = x4[:256]
    x4_edge[256:] = x4[8 * 128 :]


def inner(level, *arrays):
    return pl.pallas_call(
        inner_body,
        out_shape=(
            jax.ShapeDtypeStruct((192, 240), BF),
            jax.ShapeDtypeStruct((192, 192), BF),
            jax.ShapeDtypeStruct((192, 192), BF),
            jax.ShapeDtypeStruct((96, 768), BF),
            jax.ShapeDtypeStruct((4 * 48, 512), BF),
            jax.ShapeDtypeStruct((4 * 192, 512), BF),
            jax.ShapeDtypeStruct((4 * 192, 512), BF),
            jax.ShapeDtypeStruct((512, 256), BF),
            jax.ShapeDtypeStruct((8, 8, 256), F32),
        ),
        in_specs=[SM] + [VM] * 9,
        out_specs=(VM,) * 9,
        scratch_shapes=[
            pltpu.VMEM((16 * 48, 512), BF),
            pltpu.VMEM((14 * 192, 512), BF),
            pltpu.VMEM((12 * 192, 512), BF),
            pltpu.VMEM((10 * 128, 256), BF),
        ],
        compiler_params=pltpu.CompilerParams(vmem_limit_bytes=40 * 2**20),
        cost_estimate=pl.CostEstimate(
            flops=INNER_COST, bytes_accessed=1_000_000, transcendentals=2_000_000
        ),
    )(level, *arrays)


def outer_body(
    edges,
    w1,
    wm,
    wr,
    wo,
    columns,
    x1_edge,
    x2_edge,
    x3_edge,
    x4_edge,
    den_inner,
    base,
    slope,
    out,
    x1,
    x2,
    x3,
    x4,
    den,
):
    time_rank = lax.axis_index("tm")
    even_t = time_rank % 2 == 0
    lower = time_rank < lax.axis_size("tm") // 2
    even_s = lax.axis_index("space") % 2 == 0
    bias = columns[0][:, :1]
    gain = columns[1][:, :1]

    for y in range(4):
        u, v = edges[4 + y].astype(F32), edges[y].astype(F32)
        top = jnp.where(even_s, v, u)
        low = jnp.where(even_s, u, v)
        row_in(x1, y, even_t, top[:8], jnp.where(lower, top[8:16], top[24:]), top[16:24])
        row_in(x1, 8 + y, even_t, low[:8], jnp.where(lower, low[8:16], low[24:]), low[16:24])
    x1[4 * 48 : 8 * 48, :] = x1_edge[...]
    x4[4 * 128 : 8 * 128, :] = x4_edge[...]

    acc = [
        jnp.dot(w1[...], x1[at * 48 : at * 48 + 240, :], preferred_element_type=F32)
        for at in (0, 1, 6, 7)
    ]
    for row, k, r in (
        (0, 0, 0),
        (1, 0, 1),
        (2, 0, 2),
        (3, 1, 2),
        (4, 2, 0),
        (5, 2, 1),
        (6, 2, 2),
        (7, 3, 2),
    ):
        store_taps(x2, row, shifts(silu_half(acc[k][r * 64 : (r + 1) * 64] + bias)))

    def middle(at):
        return lambda y, m: store_taps(x3, at + y, shifts(normed(m, gain)))

    def last(at, ref, from_first, more):
        def done(y, h):
            source, row = (ref, from_first + y) if y < 2 else (more, y - 2)
            store_third(x4, at + y, source[row * 192 + 64 : row * 192 + 128, :], h)

        return done

    summed(wm[...], pieces_of((x2, 0, 4), (x2_edge, 0, 2)), middle(0))
    summed(wm[...], pieces_of((x2_edge, 2, 2), (x2, 4, 4)), middle(4))
    summed(wr[...], pieces_of((x3, 0, 4), (x3_edge, 0, 2)), last(0, x2, 2, x2_edge))
    summed(wr[...], pieces_of((x3_edge, 2, 2), (x3, 4, 4)), last(8, x2_edge, 2, x2.at[4 * 192 :]))
    out_rows(wo[...], x4, 0, den, 0)
    den[:, 4:12, :] = den_inner[...]
    out_rows(wo[...], x4, 6, den, 12)

    for v in range(8):
        out[v] = base[v] - slope[...] * den[v]


def outer(*arrays):
    return pl.pallas_call(
        outer_body,
        out_shape=jax.ShapeDtypeStruct((8, 16, 256), F32),
        in_specs=[VM] * 13,
        out_specs=VM,
        scratch_shapes=[
            pltpu.VMEM((12 * 48, 512), BF),
            pltpu.VMEM((8 * 192, 512), BF),
            pltpu.VMEM((8 * 192, 512), BF),
            pltpu.VMEM((12 * 128, 256), BF),
            pltpu.VMEM((8, 16, 256), F32),
        ],
        compiler_params=pltpu.CompilerParams(vmem_limit_bytes=40 * 2**20),
        cost_estimate=pl.CostEstimate(
            flops=4_000_000_000, bytes_accessed=1_000_000, transcendentals=1_000_000
        ),
    )(*arrays)


def order_of(count):
    return [(k + LEADER) % count for k in range(count)]


def swapped(value, axis, first, stop=None):
    count = lax.axis_size(axis)
    wrap = axis == "space"
    pairs = []
    for i in range(first, count if wrap else stop or count - 1, 2):
        j = (i + 1) % count
        pairs += [(i, j), (j, i)]
    return lax.ppermute(value, axis, pairs)


def local(
    noisy_state,
    fresh_noise,
    level_index,
    station_obs,
    obs_variance,
    station_owner,
    station_cell,
    conv_in,
    conv_mid,
    conv_res,
    conv_out,
    in_bias,
    noise_embed,
    norm_gain,
):
    even_s = lax.axis_index("space") % 2 == 0
    noisy = noisy_state.reshape(8, 16, 256)
    own, slots, columns = pack(
        level_index,
        noisy,
        station_obs,
        obs_variance.reshape(1, 128),
        station_owner.reshape(1, 128),
        station_cell.reshape(1, 128),
        in_bias.reshape(1, 64),
        noise_embed.reshape(1, 64),
        norm_gain.reshape(1, 64),
    )
    half = lax.axis_size("tm") // 2
    low = swapped(own, "tm", 0, half)
    t2 = swapped(own, "tm", 1)
    high = swapped(own, "tm", half)
    got = lax.all_to_all(
        slots, "space", 0, 0, axis_index_groups=[order_of(slots.shape[0])], tiled=True
    )

    edge = jnp.where(even_s, 12, 0)
    both = jnp.concatenate([own, low, t2, high], axis=1)
    m2 = swapped(lax.dynamic_slice_in_dim(both, 12 - edge, 4, 0), "space", 1)
    m1 = swapped(lax.dynamic_slice_in_dim(both, edge, 4, 0), "space", 0)

    edges = jnp.concatenate([m2, m1], axis=0)
    held = inner(
        level_index,
        own,
        low,
        t2,
        high,
        conv_in.transpose(0, 2, 1),
        conv_mid,
        conv_res,
        conv_out,
        columns,
    )
    base, slope = station_terms(level_index, noisy, fresh_noise.reshape(8, 16, 256), got)
    result = outer(edges, *held[:4], columns, *held[4:], base, slope)
    return result.reshape(noisy_state.shape)


def solution(mesh):
    rest = (P(),) * 7
    placed = (
        P("tm", None, "space", None),
        P("tm", None, "space", None),
        P(),
        P("tm", None, "space"),
        P("space"),
        P("space", None),
        P("space"),
    ) + rest
    return jax.shard_map(
        local, mesh=mesh, in_specs=placed, out_specs=P("tm", None, "space", None), check_vma=False
    )
```
